256 devices in a mesh: seq: 32 (over x, z_lo, core), chan: 8 (over z_hi, y).
Axes of the slice: x: 4, y: 4, z: 8 (z_hi: 2, z_lo: 4; z = z_hi * 4 + z_lo), core: 2. Of those that a mesh axis runs over, the one named last changes fastest.
Arguments:
- query_in: bfloat16 [8, 1048576], P('chan', 'seq'), may hold values from -6 to 6
- key_in: bfloat16 [8, 1048576], P('chan', 'seq'), may hold values from -6 to 6
- value_in: bfloat16 [8, 1048576], P('chan', 'seq'), may hold values from -6 to 6
- short_taps: float32 [3, 8, 3], P(None, 'chan'), may hold values from -3 to 3
- long_filter: float32 [8, 1048576], P('chan', 'seq'), may hold values from -1 to 1
- skip_gain: float32 [8], P('chan'), may hold values from -4 to 4
- w_out: bfloat16 [8, 8], replicated, may hold values from -2 to 2
Outputs:
- block_out: bfloat16 [8, 1048576], P('chan', 'seq')
The draws below stay inside these ranges and needn't reach their ends.
All inputs are finite; a program needn't handle non-finite values.
Results may differ from the reference program's by a relative error of at most 0.018.
Values may be sent and summed in bfloat16 or wider, within the bound.
No kernel may reach another device: no remote copies, remote signals or barrier semaphores. Data moves between devices by JAX's collectives and lax.ppermute only.
A program may use at most 192 MiB of HBM per device.

```python
import jax
import jax.numpy as jnp
from jax import lax

SEQ_LEN = 1048576
CHANNELS = 8


def draw_long_filter(key, part):
    key = jax.random.fold_in(key, 7)
    lowest = 0.5 / SEQ_LEN
    highest = 1.0 / 32.0
    spread = jnp.log(highest / lowest)
    positions = jnp.arange(SEQ_LEN, dtype=jnp.float32)[None, :]
    noise = jax.random.truncated_normal(jax.random.fold_in(key, 4), -4.0, 4.0, (CHANNELS, SEQ_LEN), jnp.float32)
    rates = lowest * jnp.exp(jax.random.uniform(key, (CHANNELS, 1)) * spread)
    shaped = noise
    norm = jnp.sqrt(-jnp.expm1(-2.0 * rates) / -jnp.expm1(-2.0 * rates * SEQ_LEN))
    return (0.25 * shaped * norm * jnp.exp(-rates * positions) / jnp.sqrt(2.0 * highest)).astype(jnp.float32)


def block_scale(own_key, shape, shards, smallest, largest):
    def one(position, blocks):
        draws = jax.random.uniform(jax.random.fold_in(jax.random.fold_in(own_key, 6), position), (blocks,), jnp.float32, smallest / len(shards), largest / len(shards))
        return jnp.repeat(jnp.exp(draws), shape[position] // blocks).reshape((-1,) + (1,) * (len(shape) - position - 1))

    loudness = one(*shards[0])
    for cut in shards[1:]:
        loudness = loudness * one(*cut)
    return loudness


def centred(rng, dims, scale, limit, cuts=(), kind=jnp.bfloat16):
    loudness = block_scale(rng, dims, cuts, -0.22, 0.18) if cuts else 1.0
    drawn = jax.random.normal(rng, dims, jnp.float32) * scale * loudness
    return jnp.minimum(jnp.maximum(drawn, -limit), limit).astype(kind)


def setup_inputs(seed: int = 0) -> dict:
    key_list = jax.random.split(jax.random.key(seed), 8)
    return {
        "query_in": centred(key_list[0], (CHANNELS, SEQ_LEN), 1.0, 6.0, ((0, 8), (1, 32))),
        "key_in": centred(key_list[1], (CHANNELS, SEQ_LEN), 1.0, 6.0, ((0, 8), (1, 32))),
        "value_in": centred(key_list[2], (CHANNELS, SEQ_LEN), 1.0, 6.0, ((0, 8), (1, 32))),
        "short_taps": centred(key_list[3], (3, CHANNELS, 3), 0.6, 3.0, ((1, 8),), jnp.float32),
        "long_filter": draw_long_filter(jax.random.fold_in(key_list[7], 71), 0),
        "skip_gain": centred(key_list[5], (CHANNELS,), 1.0, 4.0, ((0, 8),), jnp.float32),
        "w_out": centred(key_list[6], (CHANNELS, CHANNELS), CHANNELS ** -0.5, 2.0),
    }


def featurize(signal, weights):
    values = signal.astype(jnp.float32)
    seq_width = values.shape[1]
    padded = jnp.pad(values, ((0, 0), (2, 0)))
    summed = weights[:, 0:1] * padded[:, 2:] + weights[:, 1:2] * padded[:, 1:seq_width + 1] + weights[:, 2:3] * padded[:, 0:seq_width]
    return summed.astype(jnp.bfloat16)


def causal_conv(kv_product, long_filter):
    def one_channel(packed):
        signal, response = packed
        spectrum = jnp.fft.rfft(signal, 2 * SEQ_LEN) * jnp.fft.rfft(response, 2 * SEQ_LEN)
        return jnp.fft.irfft(spectrum, 2 * SEQ_LEN)[:SEQ_LEN]

    return lax.map(one_channel, (kv_product, long_filter))


def reference(query_in, key_in, value_in, short_taps, long_filter, skip_gain, w_out):
    q_feat = featurize(query_in, short_taps[0])
    k_feat = featurize(key_in, short_taps[1])
    v_feat = featurize(value_in, short_taps[2])
    kv_product = k_feat.astype(jnp.float32) * v_feat.astype(jnp.float32)
    convolved = causal_conv(kv_product, long_filter)
    gating = (q_feat.astype(jnp.float32) * (convolved + skip_gain[:, None] * kv_product)).astype(jnp.bfloat16)
    return jnp.dot(w_out.T, gating, preferred_element_type=jnp.float32).astype(jnp.bfloat16)
```

```python
import functools
import math

import jax
import jax.numpy as jnp
import ml_dtypes
import numpy as np
from jax import lax
from jax.experimental import pallas as pl
from jax.experimental.pallas import tpu as pltpu
from jax.sharding import PartitionSpec as P

LANES = 128
F32 = jnp.float32
BF16 = jnp.bfloat16
VMEM_LIMIT = 40 * 1024 * 1024


def tables(rows, devices):
    length = rows * LANES
    per = rows // devices
    k1 = np.arange(rows)
    first = 2.0 * math.pi * np.outer(k1 + 0.25, np.arange(rows)) / rows
    forward_first = np.stack([np.cos(first), -np.sin(first)])
    forward_first = forward_first.reshape(2, devices, per, rows).transpose(1, 0, 2, 3).reshape(2 * rows, rows)
    inverse_first = np.concatenate([np.cos(first), -np.sin(first)]).T / length
    turn = 2.0 * math.pi * np.outer(k1 + 0.25, np.arange(LANES)) / length
    turn = np.stack([np.cos(turn), np.sin(turn)])
    second = 2.0 * math.pi * np.outer(np.arange(LANES), np.arange(LANES)) / LANES
    cos, sin = np.cos(second), np.sin(second)
    forward_second = np.block([[cos, -sin], [sin, cos]])
    inverse_second = np.block([[cos, sin], [-sin, cos]])
    half = lambda values: values.astype(ml_dtypes.bfloat16)
    return (
        half(forward_first),
        turn.astype(np.float32),
        half(forward_second),
        half(inverse_second),
        half(inverse_first),
    )


def dot(left, right):
    return jnp.dot(left, right, preferred_element_type=F32)


def shifted(values, before, lane, row):
    turned = pltpu.roll(values, 1, 1)
    carried = pltpu.roll(turned, 1, 0)
    carried = jnp.where(row == 0, pltpu.roll(before, 1, 1), carried)
    return jnp.where(lane == 0, carried, turned)


def featurized(signal, before, taps_ref, stream):
    lane = lax.broadcasted_iota(jnp.int32, signal.shape, 1)
    row = lax.broadcasted_iota(jnp.int32, signal.shape, 0)
    before = jnp.broadcast_to(before, signal.shape)
    once = shifted(signal, before, lane, row)
    twice = shifted(once, pltpu.roll(before, 1, 1), lane, row)
    summed = (
        taps_ref[stream, 0] * signal + taps_ref[stream, 1] * once + taps_ref[stream, 2] * twice
    )
    return summed.astype(BF16)


def forward_kernel(devices, taps_ref, q_ref, k_ref, v_ref, rim_ref, filter_ref, first_ref, turn_ref, second_ref,
                   spectra_ref, q_feat_ref, product_ref):
    rims = rim_ref[...].astype(F32)
    rows = q_ref.shape[0]
    per = rows // devices
    q_feat_ref[...] = featurized(q_ref[...].astype(F32), rims[0:1], taps_ref, 0)
    k_feat = featurized(k_ref[...].astype(F32), rims[1:2], taps_ref, 1)
    v_feat = featurized(v_ref[...].astype(F32), rims[2:3], taps_ref, 2)
    product = k_feat.astype(F32) * v_feat.astype(F32)
    product_ref[...] = product
    signals = jnp.concatenate([product, filter_ref[...]], axis=1).astype(BF16)
    values = dot(first_ref[...], signals).reshape(devices, 2, per, 2 * LANES)
    real, imag = values[:, 0], values[:, 1]
    turn_real = turn_ref[0].reshape(devices, per, LANES)
    turn_imag = turn_ref[1].reshape(devices, per, LANES)
    packed = []
    for signal in range(2):
        lanes = slice(signal * LANES, (signal + 1) * LANES)
        a, b = real[:, :, lanes], imag[:, :, lanes]
        packed.append(
            jnp.concatenate([a * turn_real + b * turn_imag, b * turn_real - a * turn_imag], axis=2)
        )
    packed = jnp.concatenate(packed, axis=1).reshape(2 * rows, 2 * LANES).astype(BF16)
    spectra = dot(packed, second_ref[...])
    spectra_ref[...] = spectra.reshape(devices, 2 * per, 2 * LANES).astype(BF16)


def middle_kernel(devices, spectra_ref, out_ref):
    per = spectra_ref.shape[1] // 2
    blocks = []
    for p in range(devices):
        block = spectra_ref[p].astype(F32)
        blocks.append(
            (block[:per, :LANES], block[:per, LANES:], block[per:, :LANES], block[per:, LANES:])
        )
    behind_real = jnp.zeros((per, LANES), F32)
    behind_imag = behind_real
    for p in range(devices):
        real = imag = None
        for q in range(p + 1):
            a, b = blocks[q][0], blocks[q][1]
            c, d = blocks[p - q][2], blocks[p - q][3]
            term_real, term_imag = a * c - b * d, a * d + b * c
            real = term_real if real is None else real + term_real
            imag = term_imag if imag is None else imag + term_imag
        out_ref[p] = jnp.concatenate([real - behind_imag, imag + behind_real], axis=0).astype(BF16)
        behind_real, behind_imag = real, imag


def inverse_kernel(devices, skip_ref, spectra_ref, turn_ref, second_ref, first_ref, q_feat_ref, product_ref,
                   gating_ref):
    rows = q_feat_ref.shape[0]
    per = rows // devices
    packed = jnp.concatenate(
        [spectra_ref[:, :per, :].astype(F32), spectra_ref[:, per:, :].astype(F32)], axis=2
    )
    values = dot(packed.reshape(rows, 2 * LANES).astype(BF16), second_ref[...])
    a, b = values[:, :LANES], values[:, LANES:]
    turn_real, turn_imag = turn_ref[0], turn_ref[1]
    turned = jnp.concatenate([a * turn_real - b * turn_imag, a * turn_imag + b * turn_real], axis=0)
    convolved = dot(first_ref[...], turned.astype(BF16))
    gating = q_feat_ref[...].astype(F32) * (convolved + skip_ref[0] * product_ref[...])
    gating_ref[...] = gating.astype(BF16)


def project_kernel(weights_ref, gating_ref, out_ref):
    total = weights_ref[0] * gating_ref[0].astype(F32)
    for c in range(1, gating_ref.shape[0]):
        total = total + weights_ref[c] * gating_ref[c].astype(F32)
    out_ref[...] = total.astype(BF16)


SMEM = pl.BlockSpec(memory_space=pltpu.SMEM)
VMEM = pl.BlockSpec(memory_space=pltpu.VMEM)
PARAMS = pltpu.CompilerParams(vmem_limit_bytes=VMEM_LIMIT)


def on_device(devices, chans, query_in, key_in, value_in, short_taps, long_filter, skip_gain, w_out):
    width = query_in.shape[1]
    rows = width // LANES
    per = rows // devices
    forward_first, turn, forward_second, inverse_second, inverse_first = tables(rows, devices)
    query, key, value = (a.reshape(rows, LANES) for a in (query_in, key_in, value_in))
    rims = jnp.stack([a[0, -LANES:] for a in (query_in, key_in, value_in)])
    rims = lax.ppermute(rims, "seq", [(i, i + 1) for i in range(devices - 1)])
    spectra, q_feat, product = pl.pallas_call(
        functools.partial(forward_kernel, devices),
        in_specs=[SMEM] + [VMEM] * 8,
        out_specs=[VMEM] * 3,
        out_shape=[
            jax.ShapeDtypeStruct((devices, 2 * per, 2 * LANES), BF16),
            jax.ShapeDtypeStruct((rows, LANES), BF16),
            jax.ShapeDtypeStruct((rows, LANES), F32),
        ],
        compiler_params=PARAMS,
        name="forward",
    )(short_taps[:, 0], query, key, value, rims, long_filter.reshape(rows, LANES), forward_first, turn, forward_second)
    spectra = lax.all_to_all(spectra, "seq", 0, 0)
    spectra = pl.pallas_call(
        functools.partial(middle_kernel, devices),
        in_specs=[VMEM],
        out_specs=VMEM,
        out_shape=jax.ShapeDtypeStruct((devices, 2 * per, LANES), BF16),
        compiler_params=PARAMS,
        name="middle",
    )(spectra)
    spectra = lax.all_to_all(spectra, "seq", 0, 0)
    gating = pl.pallas_call(
        functools.partial(inverse_kernel, devices),
        in_specs=[SMEM] + [VMEM] * 6,
        out_specs=VMEM,
        out_shape=jax.ShapeDtypeStruct((rows, LANES), BF16),
        compiler_params=PARAMS,
        name="inverse",
    )(skip_gain, spectra, turn, inverse_second, inverse_first, q_feat, product)
    gathered = lax.all_to_all(jnp.broadcast_to(gating[None], (chans, rows, LANES)), "chan", 0, 0)
    weights = lax.dynamic_index_in_dim(w_out, lax.axis_index("chan"), axis=1, keepdims=False).astype(F32)
    out = pl.pallas_call(
        project_kernel,
        in_specs=[SMEM, VMEM],
        out_specs=VMEM,
        out_shape=jax.ShapeDtypeStruct((rows, LANES), BF16),
        compiler_params=PARAMS,
        name="project",
    )(weights, gathered)
    return out.reshape(1, width)


def solution(mesh):
    return jax.shard_map(
        functools.partial(on_device, mesh.shape["seq"], mesh.shape["chan"]),
        mesh=mesh,
        in_specs=(
            P("chan", "seq"),
            P("chan", "seq"),
            P("chan", "seq"),
            P(None, "chan", None),
            P("chan", "seq"),
            P("chan"),
            P(),
        ),
        out_specs=P("chan", "seq"),
        check_vma=False,
    )
```

```python
import functools
import math

import jax
import jax.numpy as jnp
import ml_dtypes
import numpy as np
from jax import lax
from jax.experimental import pallas as pl
from jax.experimental.pallas import tpu as pltpu
from jax.sharding import PartitionSpec as P

LANES = 128
F32 = jnp.float32
BF16 = jnp.bfloat16
VMEM_LIMIT = 40 * 1024 * 1024


def tables(rows, devices):
    length = rows * LANES
    per = rows // devices
    k1 = np.arange(rows)
    first = 2.0 * math.pi * np.outer(k1 + 0.25, np.arange(rows)) / rows
    forward_first = np.stack([np.cos(first), -np.sin(first)])
    forward_first = forward_first.reshape(2, devices, per, rows).transpose(1, 0, 2, 3).reshape(2 * rows, rows)
    inverse_first = np.concatenate([np.cos(first), -np.sin(first)]).T / length
    turn = 2.0 * math.pi * np.outer(k1 + 0.25, np.arange(LANES)) / length
    turn = np.stack([np.cos(turn), np.sin(turn)])
    second = 2.0 * math.pi * np.outer(np.arange(LANES), np.arange(LANES)) / LANES
    cos, sin = np.cos(second), np.sin(second)
    forward_second = np.block([[cos, -sin], [sin, cos]])
    inverse_second = np.block([[cos, sin], [-sin, cos]])
    basis = 2.0 * math.pi * (np.arange(per)[:, None] + 0.25 + rows * np.arange(LANES)[None, :]) / length
    basis = np.stack([np.cos(basis), -np.sin(basis)])
    half = lambda values: values.astype(ml_dtypes.bfloat16)
    return (
        half(forward_first),
        turn.astype(np.float32),
        half(forward_second),
        half(inverse_second),
        half(inverse_first),
        basis.astype(np.float32),
    )


def dot(left, right):
    return jnp.dot(left, right, preferred_element_type=F32)


def shifted(values, before, lane, row):
    turned = pltpu.roll(values, 1, 1)
    carried = pltpu.roll(turned, 1, 0)
    carried = jnp.where(row == 0, pltpu.roll(before, 1, 1), carried)
    return jnp.where(lane == 0, carried, turned)


def featurized(signal, before, taps_ref, stream):
    lane = lax.broadcasted_iota(jnp.int32, signal.shape, 1)
    row = lax.broadcasted_iota(jnp.int32, signal.shape, 0)
    before = jnp.broadcast_to(before, signal.shape)
    once = shifted(signal, before, lane, row)
    twice = shifted(once, pltpu.roll(before, 1, 1), lane, row)
    summed = (
        taps_ref[stream, 0] * signal + taps_ref[stream, 1] * once + taps_ref[stream, 2] * twice
    )
    return summed.astype(BF16)


def head_mask(shape):
    lane = lax.broadcasted_iota(jnp.int32, shape, len(shape) - 1)
    row = lax.broadcasted_iota(jnp.int32, shape, len(shape) - 2)
    return (row == 0) & (lane < 2)


def forward_kernel(devices, taps_ref, q_hbm, k_hbm, v_hbm, filter_hbm, first_hbm, turn_hbm, second_hbm,
                   message_ref, q_feat_ref, product_ref,
                   q_ref, k_ref, v_ref, filter_ref, first_ref, turn_ref, second_ref, sems):
    pairs = (
        (k_hbm, k_ref), (v_hbm, v_ref), (filter_hbm, filter_ref), (first_hbm, first_ref),
        (q_hbm, q_ref), (turn_hbm, turn_ref), (second_hbm, second_ref),
    )
    copies = [pltpu.make_async_copy(source, target, sems.at[i]) for i, (source, target) in enumerate(pairs)]
    for copy in copies:
        copy.start()
    rows = product_ref.shape[0]
    per = rows // devices
    nothing = jnp.zeros((1, LANES), F32)
    copies[0].wait()
    key = k_ref[...].astype(F32).reshape(rows, LANES)
    k_feat = featurized(key, nothing, taps_ref, 1)
    copies[1].wait()
    value = v_ref[...].astype(F32).reshape(rows, LANES)
    v_feat = featurized(value, nothing, taps_ref, 2)
    product = k_feat.astype(F32) * v_feat.astype(F32)
    product_ref[...] = product
    copies[2].wait()
    signals = jnp.concatenate([product, filter_ref[...]], axis=1).astype(BF16)
    copies[3].wait()
    values = dot(first_ref[...], signals).reshape(devices, 2, per, 2 * LANES)
    copies[4].wait()
    query = q_ref[...].astype(F32).reshape(rows, LANES)
    q_feat_ref[...] = featurized(query, nothing, taps_ref, 0)
    rims = [a[r : r + 1] for a in (key, value, query) for r in (0, rows - 1)]
    rims = jnp.concatenate(rims + [nothing, nothing], axis=0)
    copies[5].wait()
    real, imag = values[:, 0], values[:, 1]
    turn_real = turn_ref[0].reshape(devices, per, LANES)
    turn_imag = turn_ref[1].reshape(devices, per, LANES)
    packed = []
    for signal in range(2):
        lanes = slice(signal * LANES, (signal + 1) * LANES)
        a, b = real[:, :, lanes], imag[:, :, lanes]
        packed.append(
            jnp.concatenate([a * turn_real + b * turn_imag, b * turn_real - a * turn_imag], axis=2)
        )
    packed = jnp.concatenate(packed, axis=1).reshape(2 * rows, 2 * LANES).astype(BF16)
    copies[6].wait()
    spectra = dot(packed, second_ref[...]).reshape(devices, 2 * per, 2 * LANES)
    message_ref[...] = jnp.concatenate(
        [
            spectra[:, :per, :LANES],
            spectra[:, :per, LANES:],
            spectra[:, per:, :LANES],
            spectra[:, per:, LANES:],
            jnp.broadcast_to(rims[None], (devices, 8, LANES)),
        ],
        axis=1,
    ).astype(BF16)


def rounded(values):
    return values.astype(BF16).astype(F32)


def head_features(rims, taps_ref):
    lane = lax.broadcasted_iota(jnp.int32, rims.shape, 2)
    row = lax.broadcasted_iota(jnp.int32, rims.shape[1:], 0)[None]
    taps = [
        jnp.where(row < 2, taps_ref[1, j], jnp.where(row < 4, taps_ref[2, j], taps_ref[0, j])) for j in range(3)
    ]
    before = jnp.concatenate([jnp.zeros_like(rims[:1]), rims[:-1]], axis=0)
    before = pltpu.roll(before, rims.shape[1] - 1, 1)
    once, twice = pltpu.roll(rims, 1, 2), pltpu.roll(rims, 2, 2)
    with_before = (
        taps[0] * rims
        + taps[1] * jnp.where(lane < 1, pltpu.roll(before, 1, 2), once)
        + taps[2] * jnp.where(lane < 2, pltpu.roll(before, 2, 2), twice)
    )
    alone = taps[0] * rims + taps[1] * jnp.where(lane < 1, 0.0, once) + taps[2] * jnp.where(lane < 2, 0.0, twice)
    return rounded(with_before), rounded(alone)


def middle_kernel(devices, taps_ref, message_ref, basis_ref, out_ref, heads_ref, heads_scratch):
    per = (message_ref.shape[1] - 8) // 4
    own = lax.axis_index("seq")
    heads, alone = head_features(message_ref[:, 4 * per :, :].astype(F32), taps_ref)
    heads_scratch[...] = heads
    heads_ref[...] = heads_scratch[own]
    error = heads * pltpu.roll(heads, 6, 1) - alone * pltpu.roll(alone, 6, 1)
    angle = jnp.full((per, LANES), own, jnp.int32).astype(F32) * (2.0 * math.pi / (devices * LANES))
    square = angle * angle
    cos = 1.0 - square * (0.5 - square * (1.0 / 24.0))
    sin = angle * (1.0 - square * (1.0 / 6.0 - square * (1.0 / 120.0)))
    basis_real, basis_imag = basis_ref[0], basis_ref[1]
    point_real = basis_real * cos + basis_imag * sin
    point_imag = basis_imag * cos - basis_real * sin
    blocks = []
    for p in range(devices):
        block = message_ref[p].astype(F32)
        real, imag = block[:per], block[per : 2 * per]
        if p > 0:
            zeroth, first = error[p, 0:1, 0:1], error[p, 0:1, 1:2]
            real = real + (zeroth + first * point_real)
            imag = imag + first * point_imag
        blocks.append((real, imag, block[2 * per : 3 * per], block[3 * per : 4 * per]))
    behind_real = jnp.zeros((per, LANES), F32)
    behind_imag = behind_real
    for p in range(devices):
        real = imag = None
        for q in range(p + 1):
            a, b = blocks[q][0], blocks[q][1]
            c, d = blocks[p - q][2], blocks[p - q][3]
            term_real, term_imag = a * c - b * d, a * d + b * c
            real = term_real if real is None else real + term_real
            imag = term_imag if imag is None else imag + term_imag
        out_ref[p] = jnp.concatenate([real - behind_imag, imag + behind_real], axis=0).astype(BF16)
        behind_real, behind_imag = real, imag


def inverse_kernel(devices, skip_ref, spectra_ref, turn_ref, second_ref, first_ref, q_feat_ref, product_ref, heads_ref,
                   gating_ref):
    rows = q_feat_ref.shape[0]
    per = rows // devices
    packed = jnp.concatenate(
        [spectra_ref[:, :per, :].astype(F32), spectra_ref[:, per:, :].astype(F32)], axis=2
    )
    values = dot(packed.reshape(rows, 2 * LANES).astype(BF16), second_ref[...])
    a, b = values[:, :LANES], values[:, LANES:]
    turn_real, turn_imag = turn_ref[0], turn_ref[1]
    turned = jnp.concatenate([a * turn_real - b * turn_imag, a * turn_imag + b * turn_real], axis=0)
    convolved = dot(first_ref[...], turned.astype(BF16))
    head = head_mask((rows, LANES))
    heads = heads_ref[...]
    product = jnp.where(head, heads[0:1] * heads[2:3], product_ref[...])
    q_feat = jnp.where(head, heads[4:5], q_feat_ref[...].astype(F32))
    gating = (q_feat * (convolved + skip_ref[0] * product)).astype(BF16)
    for copy in range(gating_ref.shape[0]):
        gating_ref[copy] = gating


def mix_kernel(weights_ref, gating_ref, own_ref, other_ref):
    count = gating_ref.shape[0]
    own = other = None
    for c in range(count):
        gating = gating_ref[c].astype(F32)
        to_own, to_other = weights_ref[c] * gating, weights_ref[count + c] * gating
        own = to_own if own is None else own + to_own
        other = to_other if other is None else other + to_other
    own_ref[...] = own
    other_ref[...] = other.astype(BF16)


def add_kernel(own_ref, other_ref, out_ref):
    out_ref[...] = (own_ref[...] + other_ref[...].astype(F32)).reshape(out_ref.shape).astype(BF16)


SMEM = pl.BlockSpec(memory_space=pltpu.SMEM)
VMEM = pl.BlockSpec(memory_space=pltpu.VMEM)
HBM = pl.BlockSpec(memory_space=pl.ANY)
PARAMS = pltpu.CompilerParams(vmem_limit_bytes=VMEM_LIMIT)


def on_device(devices, chans, query_in, key_in, value_in, short_taps, long_filter, skip_gain, w_out):
    width = query_in.shape[1]
    rows = width // LANES
    per = rows // devices
    near = chans // 2
    forward_first, turn, forward_second, inverse_second, inverse_first, basis = tables(rows, devices)
    taps = short_taps[:, 0]
    message, q_feat, product = pl.pallas_call(
        functools.partial(forward_kernel, devices),
        in_specs=[SMEM] + [HBM] * 7,
        out_specs=[VMEM] * 3,
        out_shape=[
            jax.ShapeDtypeStruct((devices, 4 * per + 8, LANES), BF16),
            jax.ShapeDtypeStruct((rows, LANES), BF16),
            jax.ShapeDtypeStruct((rows, LANES), F32),
        ],
        scratch_shapes=[
            pltpu.VMEM((1, width), BF16),
            pltpu.VMEM((1, width), BF16),
            pltpu.VMEM((1, width), BF16),
            pltpu.VMEM((rows, LANES), F32),
            pltpu.VMEM(forward_first.shape, BF16),
            pltpu.VMEM(turn.shape, F32),
            pltpu.VMEM(forward_second.shape, BF16),
            pltpu.SemaphoreType.DMA((7,)),
        ],
        compiler_params=PARAMS,
        name="forward",
    )(taps, query_in, key_in, value_in, long_filter.reshape(rows, LANES), forward_first, turn, forward_second)
    message = lax.all_to_all(message, "seq", 0, 0)
    spectra, heads = pl.pallas_call(
        functools.partial(middle_kernel, devices),
        in_specs=[SMEM, VMEM, VMEM],
        out_specs=[VMEM] * 2,
        out_shape=[
            jax.ShapeDtypeStruct((devices, 2 * per, LANES), BF16),
            jax.ShapeDtypeStruct((8, LANES), F32),
        ],
        scratch_shapes=[pltpu.VMEM((devices, 8, LANES), F32)],
        compiler_params=PARAMS,
        name="middle",
    )(taps, message, basis)
    spectra = lax.all_to_all(spectra, "seq", 0, 0)
    gating = pl.pallas_call(
        functools.partial(inverse_kernel, devices),
        in_specs=[SMEM] + [VMEM] * 7,
        out_specs=VMEM,
        out_shape=jax.ShapeDtypeStruct((near, rows, LANES), BF16),
        compiler_params=PARAMS,
        name="inverse",
    )(skip_gain, spectra, turn, inverse_second, inverse_first, q_feat, product, heads)
    groups = [list(range(near)), list(range(near, chans))]
    gathered = lax.all_to_all(gating, "chan", 0, 0, axis_index_groups=groups)
    own_chan = lax.axis_index("chan")
    weights = lax.dynamic_slice_in_dim(w_out.astype(F32), own_chan // near * near, near, axis=0)
    weights = jnp.concatenate(
        [
            lax.dynamic_index_in_dim(weights, column, axis=1, keepdims=False)
            for column in (own_chan, (own_chan + near) % chans)
        ]
    )
    own, other = pl.pallas_call(
        mix_kernel,
        in_specs=[SMEM, VMEM],
        out_specs=[VMEM] * 2,
        out_shape=[jax.ShapeDtypeStruct((rows, LANES), F32), jax.ShapeDtypeStruct((rows, LANES), BF16)],
        compiler_params=PARAMS,
        name="mix",
    )(weights, gathered)
    other = lax.ppermute(other, "chan", [(c, (c + near) % chans) for c in range(chans)])
    return pl.pallas_call(
        add_kernel,
        in_specs=[VMEM] * 2,
        out_specs=VMEM,
        out_shape=jax.ShapeDtypeStruct((1, width), BF16),
        compiler_params=PARAMS,
        name="add",
    )(own, other)


def solution(mesh):
    return jax.shard_map(
        functools.partial(on_device, mesh.shape["seq"], mesh.shape["chan"]),
        mesh=mesh,
        in_specs=(
            P("chan", "seq"),
            P("chan", "seq"),
            P("chan", "seq"),
            P(None, "chan", None),
            P("chan", "seq"),
            P("chan"),
            P(),
        ),
        out_specs=P("chan", "seq"),
        check_vma=False,
    )
```

```python
import functools
import math

import jax
import jax.numpy as jnp
import ml_dtypes
import numpy as np
from jax import lax
from jax.experimental import pallas as pl
from jax.experimental.pallas import tpu as pltpu
from jax.sharding import PartitionSpec as P

LANES = 128
F32 = jnp.float32
BF16 = jnp.bfloat16
VMEM_LIMIT = 40 * 1024 * 1024


def tables(rows, devices):
    length = rows * LANES
    per = rows // devices
    k1 = np.arange(rows)
    first = 2.0 * math.pi * np.outer(k1 + 0.25, np.arange(rows)) / rows
    forward_first = np.stack([np.cos(first), -np.sin(first)])
    forward_first = forward_first.reshape(2, devices, per, rows).transpose(1, 0, 2, 3).reshape(2 * rows, rows)
    inverse_first = np.concatenate([np.cos(first), -np.sin(first)]).T / length
    turn = 2.0 * math.pi * np.outer(k1 + 0.25, np.arange(LANES)) / length
    turn = np.stack([np.cos(turn), np.sin(turn)])
    second = 2.0 * math.pi * np.outer(np.arange(LANES), np.arange(LANES)) / LANES
    cos, sin = np.cos(second), np.sin(second)
    forward_second = np.block([[cos, -sin], [sin, cos]])
    inverse_second = np.block([[cos, sin], [-sin, cos]])
    basis = 2.0 * math.pi * (np.arange(per)[:, None] + 0.25 + rows * np.arange(LANES)[None, :]) / length
    basis = np.stack([np.cos(basis), -np.sin(basis)])
    half = lambda values: values.astype(ml_dtypes.bfloat16)
    return (
        half(forward_first),
        turn.astype(np.float32),
        half(forward_second),
        half(inverse_second),
        half(inverse_first),
        basis.astype(np.float32),
    )


def dot(left, right):
    return jnp.dot(left, right, preferred_element_type=F32)


def shifted(values, before, lane, row):
    turned = pltpu.roll(values, 1, 1)
    carried = pltpu.roll(turned, 1, 0)
    carried = jnp.where(row == 0, pltpu.roll(before, 1, 1), carried)
    return jnp.where(lane == 0, carried, turned)


def featurized(signal, before, taps_ref, stream):
    lane = lax.broadcasted_iota(jnp.int32, signal.shape, 1)
    row = lax.broadcasted_iota(jnp.int32, signal.shape, 0)
    before = jnp.broadcast_to(before, signal.shape)
    once = shifted(signal, before, lane, row)
    twice = shifted(once, pltpu.roll(before, 1, 1), lane, row)
    summed = (
        taps_ref[stream, 0, 0] * signal + taps_ref[stream, 0, 1] * once + taps_ref[stream, 0, 2] * twice
    )
    return summed.astype(BF16)


def at_lanes(values, first):
    return pltpu.roll(values, first, 1) if first else values


def forward_kernel(devices, taps_ref, skip_ref, q_hbm, k_hbm, v_hbm, filter_hbm, first_hbm, turn_hbm, second_hbm, w_hbm,
                   message_ref, q_feat_ref, skipped_ref, scalars_ref,
                   q_ref, k_ref, v_ref, filter_ref, first_ref, turn_ref, second_ref, w_ref, sems):
    pairs = (
        (k_hbm, k_ref), (v_hbm, v_ref), (filter_hbm, filter_ref), (first_hbm, first_ref),
        (q_hbm, q_ref), (turn_hbm, turn_ref), (second_hbm, second_ref), (w_hbm, w_ref),
    )
    copies = [pltpu.make_async_copy(source, target, sems.at[i]) for i, (source, target) in enumerate(pairs)]
    for copy in copies:
        copy.start()
    rows = q_feat_ref.shape[0]
    per = rows // devices
    own, own_chan = lax.axis_index("seq"), lax.axis_index("chan")
    nothing = jnp.zeros((1, LANES), F32)
    lane = lax.broadcasted_iota(jnp.int32, (1, LANES), 1)
    for j in range(3):
        scalars_ref[j : j + 1, :] = jnp.where(
            lane < 4, taps_ref[1, 0, j], jnp.where(lane < 8, taps_ref[2, 0, j], taps_ref[0, 0, j])
        )
    scalars_ref[3:4, :] = jnp.full((1, LANES), skip_ref[0], F32)
    copies[0].wait()
    key = k_ref[...].astype(F32).reshape(rows, LANES)
    k_feat = featurized(key, nothing, taps_ref, 1)
    copies[1].wait()
    value = v_ref[...].astype(F32).reshape(rows, LANES)
    v_feat = featurized(value, nothing, taps_ref, 2)
    product = k_feat.astype(F32) * v_feat.astype(F32)
    skipped_ref[...] = skip_ref[0] * product
    copies[2].wait()
    signals = jnp.concatenate([product, filter_ref[...]], axis=1).astype(BF16)
    copies[3].wait()
    values = dot(first_ref[...], signals).reshape(devices, 2, per, 2 * LANES)
    copies[4].wait()
    query = q_ref[...].astype(F32).reshape(rows, LANES)
    q_feat_ref[...] = featurized(query, nothing, taps_ref, 0)
    edges = nothing
    for first, signal in enumerate((key, value, query)):
        ends = jnp.where(lane < 2, signal[:1], jnp.where(lane < LANES - 2, 0.0, signal[rows - 1 :]))
        edges = edges + at_lanes(ends, 4 * first)
    row = lax.broadcasted_iota(jnp.int32, (8, LANES), 0)
    edges = jnp.where(row == own % 8, jnp.broadcast_to(edges, (8, LANES)), 0.0)
    copies[5].wait()
    real, imag = values[:, 0], values[:, 1]
    turn_real = turn_ref[0].reshape(devices, per, LANES)
    turn_imag = turn_ref[1].reshape(devices, per, LANES)
    packed = []
    for signal in range(2):
        lanes = slice(signal * LANES, (signal + 1) * LANES)
        a, b = real[:, :, lanes], imag[:, :, lanes]
        packed.append(
            jnp.concatenate([a * turn_real + b * turn_imag, b * turn_real - a * turn_imag], axis=2)
        )
    packed = jnp.concatenate(packed, axis=1).reshape(2 * rows, 2 * LANES).astype(BF16)
    copies[6].wait()
    spectra = dot(packed, second_ref[...]).reshape(devices, 2 * per, 2 * LANES)
    message_ref[...] = jnp.concatenate(
        [
            spectra[:, :per, :LANES],
            spectra[:, :per, LANES:],
            spectra[:, per:, :LANES],
            spectra[:, per:, LANES:],
            jnp.broadcast_to(edges[None], (devices, 8, LANES)),
        ],
        axis=1,
    ).astype(BF16)
    copies[7].wait()
    chans = w_ref.shape[0]
    weights = w_ref[...].astype(F32)
    column = lax.broadcasted_iota(jnp.int32, weights.shape, 1)
    for i, chan in enumerate((own_chan, (own_chan + chans // 2) % chans)):
        picked = jnp.sum(jnp.where(column == chan, weights, 0.0), axis=1, keepdims=True)
        scalars_ref[8 + i * chans : 8 + (i + 1) * chans, :] = jnp.broadcast_to(picked, (chans, LANES))


def rounded(values):
    return values.astype(BF16).astype(F32)


def middle_kernel(devices, scalars_ref, message_ref, basis_ref, out_ref, heads_ref, heads_scratch, error_scratch):
    per = (message_ref.shape[1] - 8) // 4
    own = lax.axis_index("seq")
    groups = [
        sum(message_ref[p, 4 * per :, :].astype(F32) for p in range(group, group + 8)) for group in range(0, devices, 8)
    ]
    edges = jnp.concatenate(groups, axis=0)
    before = jnp.concatenate([jnp.zeros((1, LANES), F32), edges[:-1]], axis=0)
    lane = lax.broadcasted_iota(jnp.int32, edges.shape, 1)
    taps = [scalars_ref[j : j + 1, :] for j in range(3)]
    once = pltpu.roll(edges, 1, 1)
    alone = taps[0] * edges + taps[1] * jnp.where(lane % 4 == 0, 0.0, once)
    once = jnp.where(lane % 4 == 0, pltpu.roll(before, 1, 1), once)
    heads = rounded(taps[0] * edges + taps[1] * once + taps[2] * pltpu.roll(before, 2, 1))
    alone = rounded(alone)
    product = heads * pltpu.roll(heads, LANES - 4, 1)
    error = product - alone * pltpu.roll(alone, LANES - 4, 1)
    error = jnp.where(lax.broadcasted_iota(jnp.int32, edges.shape, 0) == 0, 0.0, error)
    for i in range(2):
        error_scratch[i] = jnp.broadcast_to(error[:, i : i + 1], edges.shape)
    heads_scratch[0] = pltpu.roll(heads, LANES - 8, 1)
    heads_scratch[1] = scalars_ref[3:4, :] * product
    for i in range(2):
        heads_ref[i : i + 1, :] = heads_scratch[i, pl.ds(own, 1), :]
    angle = jnp.full((per, LANES), own, jnp.int32).astype(F32) * (2.0 * math.pi / (devices * LANES))
    square = angle * angle
    cos = 1.0 - square * (0.5 - square * (1.0 / 24.0))
    sin = angle * (1.0 - square * (1.0 / 6.0 - square * (1.0 / 120.0)))
    basis_real, basis_imag = basis_ref[0], basis_ref[1]
    point_real = basis_real * cos + basis_imag * sin
    point_imag = basis_imag * cos - basis_real * sin
    blocks = []
    for p in range(devices):
        block = message_ref[p].astype(F32)
        real, imag = block[:per], block[per : 2 * per]
        if p > 0:
            first = error_scratch[1, p : p + 1, :]
            real = real + (error_scratch[0, p : p + 1, :] + first * point_real)
            imag = imag + first * point_imag
        blocks.append((real, imag, block[2 * per : 3 * per], block[3 * per : 4 * per]))
    behind_real = jnp.zeros((per, LANES), F32)
    behind_imag = behind_real
    for p in range(devices):
        real = imag = None
        for q in range(p + 1):
            a, b = blocks[q][0], blocks[q][1]
            c, d = blocks[p - q][2], blocks[p - q][3]
            term_real, term_imag = a * c - b * d, a * d + b * c
            real = term_real if real is None else real + term_real
            imag = term_imag if imag is None else imag + term_imag
        out_ref[p] = jnp.concatenate([real - behind_imag, imag + behind_real], axis=0).astype(BF16)
        behind_real, behind_imag = real, imag


def inverse_kernel(devices, spectra_ref, turn_ref, second_ref, first_ref, q_feat_ref, skipped_ref, heads_ref, gating_ref):
    rows = q_feat_ref.shape[0]
    per = rows // devices
    packed = jnp.concatenate(
        [spectra_ref[:, :per, :].astype(F32), spectra_ref[:, per:, :].astype(F32)], axis=2
    )
    values = dot(packed.reshape(rows, 2 * LANES).astype(BF16), second_ref[...])
    a, b = values[:, :LANES], values[:, LANES:]
    turn_real, turn_imag = turn_ref[0], turn_ref[1]
    turned = jnp.concatenate([a * turn_real - b * turn_imag, a * turn_imag + b * turn_real], axis=0)
    convolved = dot(first_ref[...], turned.astype(BF16))
    lane = lax.broadcasted_iota(jnp.int32, (rows, LANES), 1)
    row = lax.broadcasted_iota(jnp.int32, (rows, LANES), 0)
    head = (row == 0) & (lane < 2)
    q_feat = jnp.where(head, heads_ref[0:1, :], q_feat_ref[...].astype(F32))
    skipped = jnp.where(head, heads_ref[1:2, :], skipped_ref[...])
    gating = (q_feat * (convolved + skipped)).astype(BF16)
    for copy in range(gating_ref.shape[0]):
        gating_ref[copy] = gating


def mix_kernel(scalars_ref, gating_ref, own_ref, other_ref):
    near = gating_ref.shape[0]
    chans = 2 * near
    start = 8 + lax.axis_index("chan") // near * near
    own = other = None
    for c in range(near):
        gating = gating_ref[c].astype(F32)
        to_own = scalars_ref[pl.ds(start + c, 1), :] * gating
        to_other = scalars_ref[pl.ds(start + chans + c, 1), :] * gating
        own = to_own if own is None else own + to_own
        other = to_other if other is None else other + to_other
    own_ref[...] = own
    other_ref[...] = other.astype(BF16)


def add_kernel(own_ref, other_ref, out_ref):
    out_ref[...] = (own_ref[...] + other_ref[...].astype(F32)).reshape(out_ref.shape).astype(BF16)


SMEM = pl.BlockSpec(memory_space=pltpu.SMEM)
VMEM = pl.BlockSpec(memory_space=pltpu.VMEM)
HBM = pl.BlockSpec(memory_space=pltpu.HBM)
PARAMS = pltpu.CompilerParams(vmem_limit_bytes=VMEM_LIMIT)


def on_device(devices, chans, query_in, key_in, value_in, short_taps, long_filter, skip_gain, w_out):
    width = query_in.shape[1]
    rows = width // LANES
    per = rows // devices
    near = chans // 2
    forward_first, turn, forward_second, inverse_second, inverse_first, basis = tables(rows, devices)
    message, q_feat, skipped, scalars = pl.pallas_call(
        functools.partial(forward_kernel, devices),
        in_specs=[SMEM] * 2 + [HBM] * 8,
        out_specs=[VMEM] * 4,
        out_shape=[
            jax.ShapeDtypeStruct((devices, 4 * per + 8, LANES), BF16),
            jax.ShapeDtypeStruct((rows, LANES), BF16),
            jax.ShapeDtypeStruct((rows, LANES), F32),
            jax.ShapeDtypeStruct((8 + 2 * chans, LANES), F32),
        ],
        scratch_shapes=[
            pltpu.VMEM((1, width), BF16),
            pltpu.VMEM((1, width), BF16),
            pltpu.VMEM((1, width), BF16),
            pltpu.VMEM((rows, LANES), F32),
            pltpu.VMEM(forward_first.shape, BF16),
            pltpu.VMEM(turn.shape, F32),
            pltpu.VMEM(forward_second.shape, BF16),
            pltpu.VMEM(w_out.shape, BF16),
            pltpu.SemaphoreType.DMA((8,)),
        ],
        compiler_params=PARAMS,
        name="forward",
    )(
        short_taps,
        skip_gain,
        *(
            pltpu.with_memory_space_constraint(jnp.asarray(operand), pltpu.HBM)
            for operand in (
                query_in, key_in, value_in, long_filter.reshape(rows, LANES),
                forward_first, turn, forward_second, w_out,
            )
        ),
    )
    message = lax.all_to_all(message, "seq", 0, 0)
    spectra, heads = pl.pallas_call(
        functools.partial(middle_kernel, devices),
        in_specs=[VMEM] * 3,
        out_specs=[VMEM] * 2,
        out_shape=[
            jax.ShapeDtypeStruct((devices, 2 * per, LANES), BF16),
            jax.ShapeDtypeStruct((8, LANES), F32),
        ],
        scratch_shapes=[pltpu.VMEM((2, devices, LANES), F32)] * 2,
        compiler_params=PARAMS,
        name="middle",
    )(scalars, message, basis)
    spectra = lax.all_to_all(spectra, "seq", 0, 0)
    gating = pl.pallas_call(
        functools.partial(inverse_kernel, devices),
        in_specs=[VMEM] * 7,
        out_specs=VMEM,
        out_shape=jax.ShapeDtypeStruct((near, rows, LANES), BF16),
        compiler_params=PARAMS,
        name="inverse",
    )(spectra, turn, inverse_second, inverse_first, q_feat, skipped, heads)
    groups = [list(range(near)), list(range(near, chans))]
    gathered = lax.all_to_all(gating, "chan", 0, 0, axis_index_groups=groups)
    own, other = pl.pallas_call(
        mix_kernel,
        in_specs=[VMEM] * 2,
        out_specs=[VMEM] * 2,
        out_shape=[jax.ShapeDtypeStruct((rows, LANES), F32), jax.ShapeDtypeStruct((rows, LANES), BF16)],
        compiler_params=PARAMS,
        name="mix",
    )(scalars, gathered)
    other = lax.ppermute(other, "chan", [(c, (c + near) % chans) for c in range(chans)])
    return pl.pallas_call(
        add_kernel,
        in_specs=[VMEM] * 2,
        out_specs=VMEM,
        out_shape=jax.ShapeDtypeStruct((1, width), BF16),
        compiler_params=PARAMS,
        name="add",
    )(own, other)


def solution(mesh):
    return jax.shard_map(
        functools.partial(on_device, mesh.shape["seq"], mesh.shape["chan"]),
        mesh=mesh,
        in_specs=(
            P("chan", "seq"),
            P("chan", "seq"),
            P("chan", "seq"),
            P(None, "chan", None),
            P("chan", "seq"),
            P("chan"),
            P(),
        ),
        out_specs=P("chan", "seq"),
        check_vma=False,
    )
```

```python
import functools
import math

import jax
import jax.numpy as jnp
import ml_dtypes
import numpy as np
from jax import lax
from jax.experimental import pallas as pl
from jax.experimental.pallas import tpu as pltpu
from jax.sharding import PartitionSpec as P

LANES = 128
F32 = jnp.float32
BF16 = jnp.bfloat16
VMEM_LIMIT = 40 * 1024 * 1024


def tables(rows, devices):
    length = rows * LANES
    per = rows // devices
    k1 = np.arange(rows)
    first = 2.0 * math.pi * np.outer(k1 + 0.25, np.arange(rows)) / rows
    forward_first = np.stack([np.cos(first), -np.sin(first)])
    forward_first = forward_first.reshape(2, devices, per, rows).transpose(1, 0, 2, 3).reshape(2 * rows, rows)
    inverse_first = np.concatenate([np.cos(first), -np.sin(first)]).T / length
    turn = 2.0 * math.pi * np.outer(k1 + 0.25, np.arange(LANES)) / length
    turn = np.stack([np.cos(turn), np.sin(turn)])
    second = 2.0 * math.pi * np.outer(np.arange(LANES), np.arange(LANES)) / LANES
    cos, sin = np.cos(second), np.sin(second)
    forward_second = np.block([[cos, -sin], [sin, cos]])
    inverse_second = np.block([[cos, sin], [-sin, cos]])
    basis = 2.0 * math.pi * (np.arange(per)[:, None] + 0.25 + rows * np.arange(LANES)[None, :]) / length
    basis = np.stack([np.cos(basis), -np.sin(basis)])
    half = lambda values: values.astype(ml_dtypes.bfloat16)
    return (
        half(forward_first),
        turn.astype(np.float32),
        half(forward_second),
        half(inverse_second),
        half(inverse_first),
        basis.astype(np.float32),
    )


def dot(left, right):
    return jnp.dot(left, right, preferred_element_type=F32)


def shifted(values, before, lane, row):
    turned = pltpu.roll(values, 1, 1)
    carried = pltpu.roll(turned, 1, 0)
    carried = jnp.where(row == 0, pltpu.roll(before, 1, 1), carried)
    return jnp.where(lane == 0, carried, turned)


def featurized(signal, before, taps, stream):
    lane = lax.broadcasted_iota(jnp.int32, signal.shape, 1)
    row = lax.broadcasted_iota(jnp.int32, signal.shape, 0)
    before = jnp.broadcast_to(before, signal.shape)
    once = shifted(signal, before, lane, row)
    twice = shifted(once, pltpu.roll(before, 1, 1), lane, row)
    summed = taps[stream][0] * signal + taps[stream][1] * once + taps[stream][2] * twice
    return summed.astype(BF16)


def at_lanes(values, first):
    return pltpu.roll(values, first, 1) if first else values


def forward_kernel(devices, skip_ref, taps_hbm, q_hbm, k_hbm, v_hbm, filter_hbm, first_hbm, turn_hbm, second_hbm, w_hbm,
                   message_ref, q_feat_ref, skipped_ref, scalars_ref,
                   taps_ref, q_ref, k_ref, v_ref, filter_ref, first_ref, turn_ref, second_ref, w_ref, sems):
    pairs = (
        (taps_hbm, taps_ref),
        (k_hbm, k_ref), (v_hbm, v_ref), (filter_hbm, filter_ref), (first_hbm, first_ref),
        (q_hbm, q_ref), (turn_hbm, turn_ref), (second_hbm, second_ref), (w_hbm, w_ref),
    )
    copies = [pltpu.make_async_copy(source, target, sems.at[i]) for i, (source, target) in enumerate(pairs)]
    for copy in copies:
        copy.start()
    rows = q_feat_ref.shape[0]
    per = rows // devices
    own, own_chan = lax.axis_index("seq"), lax.axis_index("chan")
    nothing = jnp.zeros((1, LANES), F32)
    lane = lax.broadcasted_iota(jnp.int32, (1, LANES), 1)
    copies[0].wait()
    taps = [[taps_ref[stream, :, j : j + 1] for j in range(3)] for stream in range(3)]
    skip = skip_ref[0]
    for j in range(3):
        scalars_ref[j : j + 1, :] = jnp.where(lane < 4, taps[1][j], jnp.where(lane < 8, taps[2][j], taps[0][j]))
    scalars_ref[3:4, :] = jnp.full((1, LANES), skip, F32)
    copies[1].wait()
    key = k_ref[...].astype(F32).reshape(rows, LANES)
    k_feat = featurized(key, nothing, taps, 1)
    copies[2].wait()
    value = v_ref[...].astype(F32).reshape(rows, LANES)
    v_feat = featurized(value, nothing, taps, 2)
    product = k_feat.astype(F32) * v_feat.astype(F32)
    skipped_ref[...] = skip * product
    copies[3].wait()
    signals = jnp.concatenate([product, filter_ref[...]], axis=1).astype(BF16)
    copies[4].wait()
    values = dot(first_ref[...], signals).reshape(devices, 2, per, 2 * LANES)
    copies[5].wait()
    query = q_ref[...].astype(F32).reshape(rows, LANES)
    q_feat_ref[...] = featurized(query, nothing, taps, 0)
    edges = nothing
    for first, signal in enumerate((key, value, query)):
        ends = jnp.where(lane < 2, signal[:1], jnp.where(lane < LANES - 2, 0.0, signal[rows - 1 :]))
        edges = edges + at_lanes(ends, 4 * first)
    row = lax.broadcasted_iota(jnp.int32, (8, LANES), 0)
    edges = jnp.where(row == own % 8, jnp.broadcast_to(edges, (8, LANES)), 0.0)
    copies[6].wait()
    real, imag = values[:, 0], values[:, 1]
    turn_real = turn_ref[0].reshape(devices, per, LANES)
    turn_imag = turn_ref[1].reshape(devices, per, LANES)
    packed = []
    for signal in range(2):
        lanes = slice(signal * LANES, (signal + 1) * LANES)
        a, b = real[:, :, lanes], imag[:, :, lanes]
        packed.append(
            jnp.concatenate([a * turn_real + b * turn_imag, b * turn_real - a * turn_imag], axis=2)
        )
    packed = jnp.concatenate(packed, axis=1).reshape(2 * rows, 2 * LANES).astype(BF16)
    copies[7].wait()
    spectra = dot(packed, second_ref[...]).reshape(devices, 2 * per, 2 * LANES)
    message_ref[...] = jnp.concatenate(
        [
            spectra[:, :per, :LANES],
            spectra[:, :per, LANES:],
            spectra[:, per:, :LANES],
            spectra[:, per:, LANES:],
            jnp.broadcast_to(edges[None], (devices, 8, LANES)),
        ],
        axis=1,
    ).astype(BF16)
    copies[8].wait()
    chans = w_ref.shape[0]
    weights = w_ref[...].astype(F32)
    column = lax.broadcasted_iota(jnp.int32, weights.shape, 1)
    for i, chan in enumerate((own_chan, (own_chan + chans // 2) % chans)):
        picked = jnp.sum(jnp.where(column == chan, weights, 0.0), axis=1, keepdims=True)
        scalars_ref[8 + i * chans : 8 + (i + 1) * chans, :] = jnp.broadcast_to(picked, (chans, LANES))


def rounded(values):
    return values.astype(BF16).astype(F32)


def middle_kernel(devices, scalars_ref, message_ref, basis_ref, out_ref, heads_ref, heads_scratch, error_scratch):
    per = (message_ref.shape[1] - 8) // 4
    own = lax.axis_index("seq")
    groups = [
        sum(message_ref[p, 4 * per :, :].astype(F32) for p in range(group, group + 8)) for group in range(0, devices, 8)
    ]
    edges = jnp.concatenate(groups, axis=0)
    before = jnp.concatenate([jnp.zeros((1, LANES), F32), edges[:-1]], axis=0)
    lane = lax.broadcasted_iota(jnp.int32, edges.shape, 1)
    taps = [scalars_ref[j : j + 1, :] for j in range(3)]
    once = pltpu.roll(edges, 1, 1)
    alone = taps[0] * edges + taps[1] * jnp.where(lane % 4 == 0, 0.0, once)
    once = jnp.where(lane % 4 == 0, pltpu.roll(before, 1, 1), once)
    heads = rounded(taps[0] * edges + taps[1] * once + taps[2] * pltpu.roll(before, 2, 1))
    alone = rounded(alone)
    product = heads * pltpu.roll(heads, LANES - 4, 1)
    error = product - alone * pltpu.roll(alone, LANES - 4, 1)
    error = jnp.where(lax.broadcasted_iota(jnp.int32, edges.shape, 0) == 0, 0.0, error)
    for i in range(2):
        error_scratch[i] = jnp.broadcast_to(error[:, i : i + 1], edges.shape)
    heads_scratch[0] = pltpu.roll(heads, LANES - 8, 1)
    heads_scratch[1] = scalars_ref[3:4, :] * product
    for i in range(2):
        heads_ref[i : i + 1, :] = heads_scratch[i, pl.ds(own, 1), :]
    angle = jnp.full((per, LANES), own, jnp.int32).astype(F32) * (2.0 * math.pi / (devices * LANES))
    square = angle * angle
    cos = 1.0 - square * (0.5 - square * (1.0 / 24.0))
    sin = angle * (1.0 - square * (1.0 / 6.0 - square * (1.0 / 120.0)))
    basis_real, basis_imag = basis_ref[0], basis_ref[1]
    point_real = basis_real * cos + basis_imag * sin
    point_imag = basis_imag * cos - basis_real * sin
    blocks = []
    for p in range(devices):
        block = message_ref[p].astype(F32)
        real, imag = block[:per], block[per : 2 * per]
        if p > 0:
            first = error_scratch[1, p : p + 1, :]
            real = real + (error_scratch[0, p : p + 1, :] + first * point_real)
            imag = imag + first * point_imag
        blocks.append((real, imag, block[2 * per : 3 * per], block[3 * per : 4 * per]))
    behind_real = jnp.zeros((per, LANES), F32)
    behind_imag = behind_real
    for p in range(devices):
        real = imag = None
        for q in range(p + 1):
            a, b = blocks[q][0], blocks[q][1]
            c, d = blocks[p - q][2], blocks[p - q][3]
            term_real, term_imag = a * c - b * d, a * d + b * c
            real = term_real if real is None else real + term_real
            imag = term_imag if imag is None else imag + term_imag
        out_ref[p] = jnp.concatenate([real - behind_imag, imag + behind_real], axis=0).astype(BF16)
        behind_real, behind_imag = real, imag


def inverse_kernel(devices, spectra_ref, turn_ref, second_ref, first_ref, q_feat_ref, skipped_ref, heads_ref, gating_ref):
    rows = q_feat_ref.shape[0]
    per = rows // devices
    packed = jnp.concatenate(
        [spectra_ref[:, :per, :].astype(F32), spectra_ref[:, per:, :].astype(F32)], axis=2
    )
    values = dot(packed.reshape(rows, 2 * LANES).astype(BF16), second_ref[...])
    a, b = values[:, :LANES], values[:, LANES:]
    turn_real, turn_imag = turn_ref[0], turn_ref[1]
    turned = jnp.concatenate([a * turn_real - b * turn_imag, a * turn_imag + b * turn_real], axis=0)
    convolved = dot(first_ref[...], turned.astype(BF16))
    lane = lax.broadcasted_iota(jnp.int32, (rows, LANES), 1)
    row = lax.broadcasted_iota(jnp.int32, (rows, LANES), 0)
    head = (row == 0) & (lane < 2)
    q_feat = jnp.where(head, heads_ref[0:1, :], q_feat_ref[...].astype(F32))
    skipped = jnp.where(head, heads_ref[1:2, :], skipped_ref[...])
    gating = (q_feat * (convolved + skipped)).astype(BF16)
    gating_ref[...] = gating


def mix_kernel(scalars_ref, *refs):
    *gating_refs, own_ref, other_ref = refs
    near = len(gating_refs)
    chans = 2 * near
    own_chan = lax.axis_index("chan")
    start = 8 + own_chan // near * near
    own = other = None
    for step, gating_ref in enumerate(gating_refs):
        gating = gating_ref[...].astype(F32)
        row = start + (own_chan + near - step) % near
        to_own = scalars_ref[pl.ds(row, 1), :] * gating
        to_other = scalars_ref[pl.ds(row + chans, 1), :] * gating
        own = to_own if own is None else own + to_own
        other = to_other if other is None else other + to_other
    own_ref[...] = own
    other_ref[...] = other.astype(BF16)


def add_kernel(own_ref, other_ref, out_ref):
    out_ref[...] = (own_ref[...] + other_ref[...].astype(F32)).reshape(out_ref.shape).astype(BF16)


SMEM = pl.BlockSpec(memory_space=pltpu.SMEM)
VMEM = pl.BlockSpec(memory_space=pltpu.VMEM)
HBM = pl.BlockSpec(memory_space=pltpu.HBM)
PARAMS = pltpu.CompilerParams(vmem_limit_bytes=VMEM_LIMIT)


def on_device(devices, chans, query_in, key_in, value_in, short_taps, long_filter, skip_gain, w_out):
    width = query_in.shape[1]
    rows = width // LANES
    per = rows // devices
    near = chans // 2
    forward_first, turn, forward_second, inverse_second, inverse_first, basis = tables(rows, devices)
    message, q_feat, skipped, scalars = pl.pallas_call(
        functools.partial(forward_kernel, devices),
        in_specs=[SMEM] + [HBM] * 9,
        out_specs=[VMEM] * 4,
        out_shape=[
            jax.ShapeDtypeStruct((devices, 4 * per + 8, LANES), BF16),
            jax.ShapeDtypeStruct((rows, LANES), BF16),
            jax.ShapeDtypeStruct((rows, LANES), F32),
            jax.ShapeDtypeStruct((8 + 2 * chans, LANES), F32),
        ],
        scratch_shapes=[
            pltpu.VMEM(short_taps.shape, F32),
            pltpu.VMEM((1, width), BF16),
            pltpu.VMEM((1, width), BF16),
            pltpu.VMEM((1, width), BF16),
            pltpu.VMEM((rows, LANES), F32),
            pltpu.VMEM(forward_first.shape, BF16),
            pltpu.VMEM(turn.shape, F32),
            pltpu.VMEM(forward_second.shape, BF16),
            pltpu.VMEM(w_out.shape, BF16),
            pltpu.SemaphoreType.DMA((9,)),
        ],
        compiler_params=PARAMS,
        name="forward",
    )(
        skip_gain,
        *(
            pltpu.with_memory_space_constraint(jnp.asarray(operand), pltpu.HBM)
            for operand in (
                short_taps,
                query_in, key_in, value_in, long_filter.reshape(rows, LANES),
                forward_first, turn, forward_second, w_out,
            )
        ),
    )
    message = lax.all_to_all(message, "seq", 0, 0)
    spectra, heads = pl.pallas_call(
        functools.partial(middle_kernel, devices),
        in_specs=[VMEM] * 3,
        out_specs=[VMEM] * 2,
        out_shape=[
            jax.ShapeDtypeStruct((devices, 2 * per, LANES), BF16),
            jax.ShapeDtypeStruct((8, LANES), F32),
        ],
        scratch_shapes=[pltpu.VMEM((2, devices, LANES), F32)] * 2,
        compiler_params=PARAMS,
        name="middle",
    )(scalars, message, basis)
    spectra = lax.all_to_all(spectra, "seq", 0, 0)
    gating = pl.pallas_call(
        functools.partial(inverse_kernel, devices),
        in_specs=[VMEM] * 7,
        out_specs=VMEM,
        out_shape=jax.ShapeDtypeStruct((rows, LANES), BF16),
        compiler_params=PARAMS,
        name="inverse",
    )(spectra, turn, inverse_second, inverse_first, q_feat, skipped, heads)
    gathered = [gating] + [
        lax.ppermute(gating, "chan", [(c, c // near * near + (c + step) % near) for c in range(chans)])
        for step in range(1, near)
    ]
    own, other = pl.pallas_call(
        mix_kernel,
        in_specs=[VMEM] * (near + 1),
        out_specs=[VMEM] * 2,
        out_shape=[jax.ShapeDtypeStruct((rows, LANES), F32), jax.ShapeDtypeStruct((rows, LANES), BF16)],
        compiler_params=PARAMS,
        name="mix",
    )(scalars, *gathered)
    other = lax.ppermute(other, "chan", [(c, (c + near) % chans) for c in range(chans)])
    return pl.pallas_call(
        add_kernel,
        in_specs=[VMEM] * 2,
        out_specs=VMEM,
        out_shape=jax.ShapeDtypeStruct((1, width), BF16),
        compiler_params=PARAMS,
        name="add",
    )(own, other)


def solution(mesh):
    return jax.shard_map(
        functools.partial(on_device, mesh.shape["seq"], mesh.shape["chan"]),
        mesh=mesh,
        in_specs=(
            P("chan", "seq"),
            P("chan", "seq"),
            P("chan", "seq"),
            P(None, "chan", None),
            P("chan", "seq"),
            P("chan"),
            P(),
        ),
        out_specs=P("chan", "seq"),
        check_vma=False,
    )
```

```python
import functools
import math

import jax
import jax.numpy as jnp
import ml_dtypes
import numpy as np
from jax import lax
from jax.experimental import pallas as pl
from jax.experimental.pallas import tpu as pltpu
from jax.sharding import PartitionSpec as P

LANES = 128
PACK = 2
F32 = jnp.float32
BF16 = jnp.bfloat16
VMEM_LIMIT = 40 * 1024 * 1024


def tables(rows, devices):
    length = rows * LANES
    per = rows // devices
    k1 = np.arange(rows)
    first = 2.0 * math.pi * np.outer(k1 + 0.25, np.arange(rows)) / rows
    forward_first = np.stack([np.cos(first), -np.sin(first)])
    forward_first = forward_first.reshape(2, devices, per, rows).transpose(1, 0, 2, 3).reshape(2 * rows, rows)
    inverse_first = np.concatenate([np.cos(first), -np.sin(first)]).T / length
    turn = 2.0 * math.pi * np.outer(k1 + 0.25, np.arange(LANES)) / length
    turn = np.stack([np.cos(turn), np.sin(turn)])
    second = 2.0 * math.pi * np.outer(np.arange(LANES), np.arange(LANES)) / LANES
    cos, sin = np.cos(second), np.sin(second)
    forward_second = np.block([[cos, -sin], [sin, cos]])
    inverse_second = np.block([[cos, sin], [-sin, cos]])
    basis = 2.0 * math.pi * (np.arange(per)[:, None] + 0.25 + rows * np.arange(LANES)[None, :]) / length
    basis = np.stack([np.cos(basis), -np.sin(basis)])
    half = lambda values: values.astype(ml_dtypes.bfloat16)
    return (
        half(forward_first),
        turn.astype(np.float32),
        half(forward_second),
        half(inverse_second),
        half(inverse_first),
        basis.astype(np.float32),
    )


def dot(left, right):
    return jnp.dot(left, right, preferred_element_type=F32)


def shifted(values, before, lane, row):
    turned = pltpu.roll(values, 1, 1)
    carried = pltpu.roll(turned, 1, 0)
    carried = jnp.where(row == 0, pltpu.roll(before, 1, 1), carried)
    return jnp.where(lane == 0, carried, turned)


def featurized(signal, before, taps, stream):
    lane = lax.broadcasted_iota(jnp.int32, signal.shape, 1)
    row = lax.broadcasted_iota(jnp.int32, signal.shape, 0)
    before = jnp.broadcast_to(before, signal.shape)
    once = shifted(signal, before, lane, row)
    twice = shifted(once, pltpu.roll(before, 1, 1), lane, row)
    summed = taps[stream][0] * signal + taps[stream][1] * once + taps[stream][2] * twice
    return summed.astype(BF16)


def at_lanes(values, first):
    return pltpu.roll(values, first, 1) if first else values


def forward_kernel(devices, taps_hbm, q_hbm, k_hbm, v_hbm, filter_hbm, first_hbm, turn_hbm, second_hbm, w_hbm,
                   message_ref, q_feat_ref, skipped_ref, scalars_ref,
                   taps_ref, q_ref, k_ref, v_ref, filter_ref, first_ref, turn_ref, second_ref, w_ref, sems):
    pairs = (
        (taps_hbm, taps_ref),
        (k_hbm, k_ref), (v_hbm, v_ref), (filter_hbm, filter_ref), (first_hbm, first_ref),
        (q_hbm, q_ref), (turn_hbm, turn_ref), (second_hbm, second_ref), (w_hbm, w_ref),
    )
    copies = [pltpu.make_async_copy(source, target, sems.at[i]) for i, (source, target) in enumerate(pairs)]
    for copy in copies:
        copy.start()
    rows = q_feat_ref.shape[0]
    per = rows // devices
    own, own_chan = lax.axis_index("seq"), lax.axis_index("chan")
    nothing = jnp.zeros((1, LANES), F32)
    lane = lax.broadcasted_iota(jnp.int32, (1, LANES), 1)
    copies[0].wait()
    taps = [[taps_ref[stream, :, j : j + 1] for j in range(3)] for stream in range(3)]
    for j in range(3):
        scalars_ref[j : j + 1, :] = jnp.where(lane < 4, taps[1][j], jnp.where(lane < 8, taps[2][j], taps[0][j]))
    copies[1].wait()
    key = k_ref[...].astype(F32).reshape(rows, LANES)
    k_feat = featurized(key, nothing, taps, 1)
    copies[2].wait()
    value = v_ref[...].astype(F32).reshape(rows, LANES)
    v_feat = featurized(value, nothing, taps, 2)
    product = k_feat.astype(F32) * v_feat.astype(F32)
    skipped_ref[...] = product
    copies[3].wait()
    signals = jnp.concatenate([product, filter_ref[...]], axis=1).astype(BF16)
    copies[4].wait()
    values = dot(first_ref[...], signals).reshape(devices, 2, per, 2 * LANES)
    copies[5].wait()
    query = q_ref[...].astype(F32).reshape(rows, LANES)
    q_feat_ref[...] = featurized(query, nothing, taps, 0)
    edges = nothing
    for first, signal in enumerate((key, value, query)):
        ends = jnp.where(lane < 2, signal[:1], jnp.where(lane < LANES - 2, 0.0, signal[rows - 1 :]))
        edges = edges + at_lanes(ends, 4 * first)
    row = lax.broadcasted_iota(jnp.int32, (8, LANES), 0)
    edges = jnp.where(row == 0, jnp.broadcast_to(edges, (8, LANES)), 0.0)[:PACK]
    copies[6].wait()
    real, imag = values[:, 0], values[:, 1]
    turn_real = turn_ref[0].reshape(devices, per, LANES)
    turn_imag = turn_ref[1].reshape(devices, per, LANES)
    packed = []
    for signal in range(2):
        lanes = slice(signal * LANES, (signal + 1) * LANES)
        a, b = real[:, :, lanes], imag[:, :, lanes]
        packed.append(
            jnp.concatenate([a * turn_real + b * turn_imag, b * turn_real - a * turn_imag], axis=2)
        )
    packed = jnp.concatenate(packed, axis=1).reshape(2 * rows, 2 * LANES).astype(BF16)
    copies[7].wait()
    spectra = dot(packed, second_ref[...]).reshape(devices, 2 * per, 2 * LANES)
    spectra = jnp.concatenate(
        [
            spectra[:, :per, :LANES],
            spectra[:, :per, LANES:],
            spectra[:, per:, :LANES],
            spectra[:, per:, LANES:],
        ],
        axis=1,
    ).astype(BF16)
    packs = 4 * per // PACK
    message_ref[:, :packs] = spectra.reshape(devices, packs, PACK, LANES)
    message_ref[:, packs] = jnp.broadcast_to(edges.astype(BF16)[None], (devices, PACK, LANES))
    copies[8].wait()
    chans = w_ref.shape[0]
    weights = w_ref[...].astype(F32)
    column = lax.broadcasted_iota(jnp.int32, weights.shape, 1)
    for i, chan in enumerate((own_chan, (own_chan + chans // 2) % chans)):
        picked = jnp.sum(jnp.where(column == chan, weights, 0.0), axis=1, keepdims=True)
        scalars_ref[8 + i * chans : 8 + (i + 1) * chans, :] = jnp.broadcast_to(picked, (chans, LANES))


def rounded(values):
    return values.astype(BF16).astype(F32)


def middle_kernel(devices, skip_ref, scalars_ref, message_ref, basis_ref, out_ref, heads_ref, heads_scratch, error_scratch, aligned_ref):
    pitch = message_ref.shape[0] // devices
    per = (pitch - PACK) // 4
    message = message_ref[...].astype(F32)
    own = lax.axis_index("seq")
    edges = jnp.concatenate([message[(p + 1) * pitch - PACK : (p + 1) * pitch - PACK + 1] for p in range(devices)], axis=0)
    before = jnp.concatenate([jnp.zeros((1, LANES), F32), edges[:-1]], axis=0)
    lane = lax.broadcasted_iota(jnp.int32, edges.shape, 1)
    taps = [scalars_ref[j : j + 1, :] for j in range(3)]
    once = pltpu.roll(edges, 1, 1)
    alone = taps[0] * edges + taps[1] * jnp.where(lane % 4 == 0, 0.0, once)
    once = jnp.where(lane % 4 == 0, pltpu.roll(before, 1, 1), once)
    heads = rounded(taps[0] * edges + taps[1] * once + taps[2] * pltpu.roll(before, 2, 1))
    alone = rounded(alone)
    product = heads * pltpu.roll(heads, LANES - 4, 1)
    error = product - alone * pltpu.roll(alone, LANES - 4, 1)
    error = jnp.where(lax.broadcasted_iota(jnp.int32, edges.shape, 0) == 0, 0.0, error)
    for i in range(2):
        error_scratch[i] = jnp.broadcast_to(error[:, i : i + 1], edges.shape)
    heads_scratch[0] = pltpu.roll(heads, LANES - 8, 1)
    heads_scratch[1] = product
    for i in range(2):
        heads_ref[i : i + 1, :] = heads_scratch[i, pl.ds(own, 1), :]
    heads_ref[2:3, :] = jnp.full((1, LANES), skip_ref[0], F32)
    angle = jnp.full((per, LANES), own, jnp.int32).astype(F32) * (2.0 * math.pi / (devices * LANES))
    square = angle * angle
    cos = 1.0 - square * (0.5 - square * (1.0 / 24.0))
    sin = angle * (1.0 - square * (1.0 / 6.0 - square * (1.0 / 120.0)))
    basis_real, basis_imag = basis_ref[0], basis_ref[1]
    point_real = basis_real * cos + basis_imag * sin
    point_imag = basis_imag * cos - basis_real * sin
    blocks = []
    for p in range(devices):
        aligned_ref[p] = message[p * pitch : p * pitch + 4 * per]
    for p in range(devices):
        block = aligned_ref[p]
        real, imag = block[:per], block[per : 2 * per]
        if p > 0:
            first = error_scratch[1, p : p + 1, :]
            real = real + (error_scratch[0, p : p + 1, :] + first * point_real)
            imag = imag + first * point_imag
        c, d = block[2 * per : 3 * per], block[3 * per : 4 * per]
        blocks.append((real + imag, real, imag, c, d - c, c + d))
    behind_real = jnp.zeros((per, LANES), F32)
    behind_imag = behind_real
    for p in range(devices):
        sums = [None] * 3
        for q in range(p + 1):
            for i in range(3):
                term = blocks[q][i] * blocks[p - q][3 + i]
                sums[i] = term if sums[i] is None else sums[i] + term
        real, imag = sums[0] - sums[2], sums[0] + sums[1]
        out_ref[p] = jnp.concatenate([real - behind_imag, imag + behind_real], axis=0).astype(BF16)
        behind_real, behind_imag = real, imag


def inverse_kernel(devices, spectra_ref, turn_ref, second_ref, first_ref, q_feat_ref, skipped_ref, heads_ref, gating_ref):
    rows = q_feat_ref.shape[0]
    per = rows // devices
    packed = jnp.concatenate(
        [spectra_ref[:, :per, :].astype(F32), spectra_ref[:, per:, :].astype(F32)], axis=2
    )
    values = dot(packed.reshape(rows, 2 * LANES).astype(BF16), second_ref[...])
    a, b = values[:, :LANES], values[:, LANES:]
    turn_real, turn_imag = turn_ref[0], turn_ref[1]
    turned = jnp.concatenate([a * turn_real - b * turn_imag, a * turn_imag + b * turn_real], axis=0)
    convolved = dot(first_ref[...], turned.astype(BF16))
    lane = lax.broadcasted_iota(jnp.int32, (rows, LANES), 1)
    row = lax.broadcasted_iota(jnp.int32, (rows, LANES), 0)
    head = (row == 0) & (lane < 2)
    q_feat = jnp.where(head, heads_ref[0:1, :], q_feat_ref[...].astype(F32))
    skipped = heads_ref[2:3, :] * jnp.where(head, heads_ref[1:2, :], skipped_ref[...])
    gating = (q_feat * (convolved + skipped)).astype(BF16)
    gating_ref[...] = gating


def mix_kernel(scalars_ref, *refs):
    *gating_refs, own_ref, other_ref = refs
    near = len(gating_refs)
    chans = 2 * near
    own_chan = lax.axis_index("chan")
    start = 8 + own_chan // near * near
    own = other = None
    for step, gating_ref in enumerate(gating_refs):
        gating = gating_ref[...].astype(F32)
        row = start + (own_chan + near - step) % near
        to_own = scalars_ref[pl.ds(row, 1), :] * gating
        to_other = scalars_ref[pl.ds(row + chans, 1), :] * gating
        own = to_own if own is None else own + to_own
        other = to_other if other is None else other + to_other
    own_ref[...] = own
    other_ref[...] = other.astype(BF16)


def add_kernel(own_ref, other_ref, out_ref):
    out_ref[...] = (own_ref[...] + other_ref[...].astype(F32)).reshape(out_ref.shape).astype(BF16)


SMEM = pl.BlockSpec(memory_space=pltpu.SMEM)
VMEM = pl.BlockSpec(memory_space=pltpu.VMEM)
HBM = pl.BlockSpec(memory_space=pltpu.HBM)
PARAMS = pltpu.CompilerParams(vmem_limit_bytes=VMEM_LIMIT)


def on_device(devices, chans, query_in, key_in, value_in, short_taps, long_filter, skip_gain, w_out):
    width = query_in.shape[1]
    rows = width // LANES
    per = rows // devices
    near = chans // 2
    forward_first, turn, forward_second, inverse_second, inverse_first, basis = tables(rows, devices)
    message, q_feat, skipped, scalars = pl.pallas_call(
        functools.partial(forward_kernel, devices),
        in_specs=[HBM] * 9,
        out_specs=[VMEM] * 4,
        out_shape=[
            jax.ShapeDtypeStruct((devices, 4 * per // PACK + 1, PACK, LANES), BF16),
            jax.ShapeDtypeStruct((rows, LANES), BF16),
            jax.ShapeDtypeStruct((rows, LANES), F32),
            jax.ShapeDtypeStruct((8 + 2 * chans, LANES), F32),
        ],
        scratch_shapes=[
            pltpu.VMEM(short_taps.shape, F32),
            pltpu.VMEM((1, width), BF16),
            pltpu.VMEM((1, width), BF16),
            pltpu.VMEM((1, width), BF16),
            pltpu.VMEM((rows, LANES), F32),
            pltpu.VMEM(forward_first.shape, BF16),
            pltpu.VMEM(turn.shape, F32),
            pltpu.VMEM(forward_second.shape, BF16),
            pltpu.VMEM(w_out.shape, BF16),
            pltpu.SemaphoreType.DMA((9,)),
        ],
        compiler_params=PARAMS,
        name="forward",
    )(
        *(
            pltpu.with_memory_space_constraint(jnp.asarray(operand), pltpu.HBM)
            for operand in (
                short_taps,
                query_in, key_in, value_in, long_filter.reshape(rows, LANES),
                forward_first, turn, forward_second, w_out,
            )
        ),
    )
    message = lax.all_to_all(message, "seq", 0, 0)
    spectra, heads = pl.pallas_call(
        functools.partial(middle_kernel, devices),
        in_specs=[SMEM] + [VMEM] * 3,
        out_specs=[VMEM] * 2,
        out_shape=[
            jax.ShapeDtypeStruct((devices, 2 * per, LANES), BF16),
            jax.ShapeDtypeStruct((8, LANES), F32),
        ],
        scratch_shapes=[pltpu.VMEM((2, devices, LANES), F32)] * 2 + [pltpu.VMEM((devices, 4 * per, LANES), F32)],
        compiler_params=PARAMS,
        name="middle",
    )(skip_gain, scalars, message.reshape(-1, LANES), basis)
    spectra = lax.all_to_all(spectra, "seq", 0, 0)
    gating = pl.pallas_call(
        functools.partial(inverse_kernel, devices),
        in_specs=[VMEM] * 7,
        out_specs=VMEM,
        out_shape=jax.ShapeDtypeStruct((rows, LANES), BF16),
        compiler_params=PARAMS,
        name="inverse",
    )(spectra, turn, inverse_second, inverse_first, q_feat, skipped, heads)
    gathered = [gating] + [
        lax.ppermute(gating, "chan", [(c, c // near * near + (c + step) % near) for c in range(chans)])
        for step in range(1, near)
    ]
    own, other = pl.pallas_call(
        mix_kernel,
        in_specs=[VMEM] * (near + 1),
        out_specs=[VMEM] * 2,
        out_shape=[jax.ShapeDtypeStruct((rows, LANES), F32), jax.ShapeDtypeStruct((rows, LANES), BF16)],
        compiler_params=PARAMS,
        name="mix",
    )(scalars, *gathered)
    other = lax.ppermute(other, "chan", [(c, (c + near) % chans) for c in range(chans)])
    return pl.pallas_call(
        add_kernel,
        in_specs=[VMEM] * 2,
        out_specs=VMEM,
        out_shape=jax.ShapeDtypeStruct((1, width), BF16),
        compiler_params=PARAMS,
        name="add",
    )(own, other)


def solution(mesh):
    return jax.shard_map(
        functools.partial(on_device, mesh.shape["seq"], mesh.shape["chan"]),
        mesh=mesh,
        in_specs=(
            P("chan", "seq"),
            P("chan", "seq"),
            P("chan", "seq"),
            P(None, "chan", None),
            P("chan", "seq"),
            P("chan"),
            P(),
        ),
        out_specs=P("chan", "seq"),
        check_vma=False,
    )
```

```python
import functools
import math

import jax
import jax.numpy as jnp
import ml_dtypes
import numpy as np
from jax import lax
from jax.experimental import pallas as pl
from jax.experimental.pallas import tpu as pltpu
from jax.sharding import PartitionSpec as P

LANES = 128
PACK = 2
CHUNKS = 2
F32 = jnp.float32
BF16 = jnp.bfloat16
VMEM_LIMIT = 40 * 1024 * 1024


def tables(rows, devices):
    length = rows * LANES
    per = rows // devices
    k1 = np.arange(rows)
    first = 2.0 * math.pi * np.outer(k1 + 0.25, np.arange(rows)) / rows
    forward_first = np.stack([np.cos(first), -np.sin(first)])
    forward_first = forward_first.reshape(2, devices, per, rows).transpose(1, 0, 2, 3).reshape(2 * rows, rows)
    inverse_first = np.concatenate([np.cos(first), -np.sin(first)]).T / length
    turn = 2.0 * math.pi * np.outer(k1 + 0.25, np.arange(LANES)) / length
    turn = np.stack([np.cos(turn), np.sin(turn)])
    second = 2.0 * math.pi * np.outer(np.arange(LANES), np.arange(LANES)) / LANES
    cos, sin = np.cos(second), np.sin(second)
    forward_second = np.block([[cos, -sin], [sin, cos]])
    inverse_second = np.block([[cos, sin], [-sin, cos]])
    basis = 2.0 * math.pi * (np.arange(per)[:, None] + 0.25 + rows * np.arange(LANES)[None, :]) / length
    basis = np.stack([np.cos(basis), -np.sin(basis)])
    half = lambda values: values.astype(ml_dtypes.bfloat16)
    return (
        half(forward_first),
        turn.astype(np.float32),
        half(forward_second),
        half(inverse_second),
        half(inverse_first),
        basis.astype(np.float32),
    )


def dot(left, right):
    return jnp.dot(left, right, preferred_element_type=F32)


def moved_on(values, lane, row):
    turned = pltpu.roll(values, 1, 1)
    carried = jnp.where(row == 0, 0.0, pltpu.roll(turned, 1, 0))
    return jnp.where(lane == 0, carried, turned)


def featurized(signal, taps, stream):
    lane = lax.broadcasted_iota(jnp.int32, signal.shape, 1)
    row = lax.broadcasted_iota(jnp.int32, signal.shape, 0)
    once = moved_on(signal, lane, row)
    twice = moved_on(once, lane, row)
    summed = taps[stream][0] * signal + taps[stream][1] * once + taps[stream][2] * twice
    return summed.astype(BF16)


def at_lanes(values, first):
    return pltpu.roll(values, first, 1) if first else values


def forward_kernel(devices, taps_hbm, k_hbm, v_hbm, q_hbm, filter_hbm, first_hbm, turn_hbm, second_hbm,
                   message_hbm, product_ref,
                   taps_ref, k_ref, v_ref, q_ref, filter_ref, first_ref, turn_ref, second_ref, sems, message_ref, out_sems):
    width = k_hbm.shape[1]
    pairs = (
        (taps_hbm, taps_ref),
        (k_hbm, k_ref),
        (v_hbm, v_ref),
        (filter_hbm, filter_ref),
        (first_hbm, first_ref),
        (q_hbm.at[:, pl.ds(0, LANES)], q_ref.at[0]),
        (q_hbm.at[:, pl.ds(width - LANES, LANES)], q_ref.at[1]),
        (turn_hbm, turn_ref),
        (second_hbm, second_ref),
    )
    copies = [pltpu.make_async_copy(source, target, sems.at[i]) for i, (source, target) in enumerate(pairs)]
    for copy in copies:
        copy.start()
    rows = product_ref.shape[0]
    per = rows // devices
    lane = lax.broadcasted_iota(jnp.int32, (1, LANES), 1)
    copies[0].wait()
    taps = [[taps_ref[stream, :, j : j + 1] for j in range(3)] for stream in range(3)]
    for copy in copies[1:]:
        copy.wait()
    key = k_ref[...].astype(F32).reshape(rows, LANES)
    k_feat = featurized(key, taps, 1)
    value = v_ref[...].astype(F32).reshape(rows, LANES)
    v_feat = featurized(value, taps, 2)
    product = k_feat.astype(F32) * v_feat.astype(F32)
    product_ref[...] = product
    signals = jnp.concatenate([product, filter_ref[...]], axis=1).astype(BF16)
    values = dot(first_ref[...], signals).reshape(devices, 2, per, 2 * LANES)
    edges = jnp.zeros((1, LANES), F32)
    pieces = ((key[:1], key[rows - 1 :]), (value[:1], value[rows - 1 :]), (q_ref[0].astype(F32), q_ref[1].astype(F32)))
    for i, (head, tail) in enumerate(pieces):
        ends = jnp.where(lane < 2, head, jnp.where(lane < LANES - 2, 0.0, tail))
        edges = edges + at_lanes(ends, 4 * i)
    row = lax.broadcasted_iota(jnp.int32, (8, LANES), 0)
    edges = jnp.where(row == 0, jnp.broadcast_to(edges, (8, LANES)), 0.0)[:PACK].astype(BF16)
    packs = 4 * per // PACK
    count = devices // CHUNKS
    for chunk in range(CHUNKS):
        part = slice(chunk * count, (chunk + 1) * count)
        lines = slice(chunk * count * per, (chunk + 1) * count * per)
        real, imag = values[part, 0], values[part, 1]
        turn_real = turn_ref[0, lines].reshape(count, per, LANES)
        turn_imag = turn_ref[1, lines].reshape(count, per, LANES)
        packed = []
        for signal in range(2):
            lanes = slice(signal * LANES, (signal + 1) * LANES)
            a, b = real[:, :, lanes], imag[:, :, lanes]
            packed.append(
                jnp.concatenate([a * turn_real + b * turn_imag, b * turn_real - a * turn_imag], axis=2)
            )
        packed = jnp.concatenate(packed, axis=1).reshape(2 * count * per, 2 * LANES).astype(BF16)
        spectra = dot(packed, second_ref[...]).reshape(count, 2 * per, 2 * LANES)
        spectra = jnp.concatenate(
            [
                spectra[:, :per, :LANES],
                spectra[:, :per, LANES:],
                spectra[:, per:, :LANES],
                spectra[:, per:, LANES:],
            ],
            axis=1,
        ).astype(BF16)
        message_ref[part, :packs] = spectra.reshape(count, packs, PACK, LANES)
        message_ref[part, packs] = jnp.broadcast_to(edges[None], (count, PACK, LANES))
        copies.append(pltpu.make_async_copy(message_ref.at[part], message_hbm.at[part], out_sems.at[chunk]))
        copies[-1].start()
    for copy in copies[9:]:
        copy.wait()


def side_kernel(devices, taps_ref, q_ref, w_ref, q_feat_ref, scalars_ref):
    rows = q_feat_ref.shape[0]
    own_chan = lax.axis_index("chan")
    lane = lax.broadcasted_iota(jnp.int32, (1, LANES), 1)
    taps = [[taps_ref[stream, :, j : j + 1] for j in range(3)] for stream in range(3)]
    for j in range(3):
        scalars_ref[j : j + 1, :] = jnp.where(lane < 4, taps[1][j], jnp.where(lane < 8, taps[2][j], taps[0][j]))
    query = q_ref[...].astype(F32).reshape(rows, LANES)
    q_feat_ref[...] = featurized(query, taps, 0)
    chans = w_ref.shape[0]
    weights = w_ref[...].astype(F32)
    column = lax.broadcasted_iota(jnp.int32, weights.shape, 1)
    for i, chan in enumerate((own_chan, (own_chan + chans // 2) % chans)):
        picked = jnp.sum(jnp.where(column == chan, weights, 0.0), axis=1, keepdims=True)
        scalars_ref[8 + i * chans : 8 + (i + 1) * chans, :] = jnp.broadcast_to(picked, (chans, LANES))


def rounded(values):
    return values.astype(BF16).astype(F32)


def middle_kernel(devices, skip_ref, scalars_ref, message_ref, basis_ref, out_ref, heads_ref, heads_scratch, error_scratch, aligned_ref):
    pitch = message_ref.shape[0] // devices
    per = (pitch - PACK) // 4
    message = message_ref[...].astype(F32)
    own = lax.axis_index("seq")
    edges = jnp.concatenate([message[(p + 1) * pitch - PACK : (p + 1) * pitch - PACK + 1] for p in range(devices)], axis=0)
    before = jnp.concatenate([jnp.zeros((1, LANES), F32), edges[:-1]], axis=0)
    lane = lax.broadcasted_iota(jnp.int32, edges.shape, 1)
    taps = [scalars_ref[j : j + 1, :] for j in range(3)]
    once = pltpu.roll(edges, 1, 1)
    alone = taps[0] * edges + taps[1] * jnp.where(lane % 4 == 0, 0.0, once)
    once = jnp.where(lane % 4 == 0, pltpu.roll(before, 1, 1), once)
    heads = rounded(taps[0] * edges + taps[1] * once + taps[2] * pltpu.roll(before, 2, 1))
    alone = rounded(alone)
    product = heads * pltpu.roll(heads, LANES - 4, 1)
    error = product - alone * pltpu.roll(alone, LANES - 4, 1)
    error = jnp.where(lax.broadcasted_iota(jnp.int32, edges.shape, 0) == 0, 0.0, error)
    for i in range(2):
        error_scratch[i] = jnp.broadcast_to(error[:, i : i + 1], edges.shape)
    heads_scratch[0] = pltpu.roll(heads, LANES - 8, 1)
    heads_scratch[1] = product
    for i in range(2):
        heads_ref[i : i + 1, :] = heads_scratch[i, pl.ds(own, 1), :]
    heads_ref[2:3, :] = jnp.full((1, LANES), skip_ref[0], F32)
    angle = jnp.full((per, LANES), own, jnp.int32).astype(F32) * (2.0 * math.pi / (devices * LANES))
    square = angle * angle
    cos = 1.0 - square * (0.5 - square * (1.0 / 24.0))
    sin = angle * (1.0 - square * (1.0 / 6.0 - square * (1.0 / 120.0)))
    basis_real, basis_imag = basis_ref[0], basis_ref[1]
    point_real = basis_real * cos + basis_imag * sin
    point_imag = basis_imag * cos - basis_real * sin
    blocks = []
    for p in range(devices):
        aligned_ref[p] = message[p * pitch : p * pitch + 4 * per]
    for p in range(devices):
        block = aligned_ref[p]
        real, imag = block[:per], block[per : 2 * per]
        if p > 0:
            first = error_scratch[1, p : p + 1, :]
            real = real + (error_scratch[0, p : p + 1, :] + first * point_real)
            imag = imag + first * point_imag
        c, d = block[2 * per : 3 * per], block[3 * per : 4 * per]
        blocks.append((real + imag, real, imag, c, d - c, c + d))
    behind_real = jnp.zeros((per, LANES), F32)
    behind_imag = behind_real
    for p in range(devices):
        sums = [None] * 3
        for q in range(p + 1):
            for i in range(3):
                term = blocks[q][i] * blocks[p - q][3 + i]
                sums[i] = term if sums[i] is None else sums[i] + term
        real, imag = sums[0] - sums[2], sums[0] + sums[1]
        out_ref[p] = jnp.concatenate([real - behind_imag, imag + behind_real], axis=0).astype(BF16)
        behind_real, behind_imag = real, imag


def inverse_kernel(devices, spectra_ref, turn_ref, second_ref, first_ref, q_feat_ref, skipped_ref, heads_ref, gating_ref):
    rows = q_feat_ref.shape[0]
    per = rows // devices
    packed = jnp.concatenate(
        [spectra_ref[:, :per, :].astype(F32), spectra_ref[:, per:, :].astype(F32)], axis=2
    )
    values = dot(packed.reshape(rows, 2 * LANES).astype(BF16), second_ref[...])
    a, b = values[:, :LANES], values[:, LANES:]
    turn_real, turn_imag = turn_ref[0], turn_ref[1]
    turned = jnp.concatenate([a * turn_real - b * turn_imag, a * turn_imag + b * turn_real], axis=0)
    convolved = dot(first_ref[...], turned.astype(BF16))
    lane = lax.broadcasted_iota(jnp.int32, (rows, LANES), 1)
    row = lax.broadcasted_iota(jnp.int32, (rows, LANES), 0)
    head = (row == 0) & (lane < 2)
    q_feat = jnp.where(head, heads_ref[0:1, :], q_feat_ref[...].astype(F32))
    skipped = heads_ref[2:3, :] * jnp.where(head, heads_ref[1:2, :], skipped_ref[...])
    gating = (q_feat * (convolved + skipped)).astype(BF16)
    gating_ref[...] = gating


def mix_kernel(scalars_ref, *refs):
    *gating_refs, own_ref, other_ref = refs
    near = len(gating_refs)
    chans = 2 * near
    own_chan = lax.axis_index("chan")
    start = 8 + own_chan // near * near
    own = other = None
    for step, gating_ref in enumerate(gating_refs):
        gating = gating_ref[...].astype(F32)
        row = start + (own_chan + near - step) % near
        to_own = scalars_ref[pl.ds(row, 1), :] * gating
        to_other = scalars_ref[pl.ds(row + chans, 1), :] * gating
        own = to_own if own is None else own + to_own
        other = to_other if other is None else other + to_other
    own_ref[...] = own
    other_ref[...] = other.astype(BF16)


def add_kernel(own_ref, other_ref, out_ref):
    out_ref[...] = (own_ref[...] + other_ref[...].astype(F32)).reshape(out_ref.shape).astype(BF16)


SMEM = pl.BlockSpec(memory_space=pltpu.SMEM)
VMEM = pl.BlockSpec(memory_space=pltpu.VMEM)
HBM = pl.BlockSpec(memory_space=pltpu.HBM)
PARAMS = pltpu.CompilerParams(vmem_limit_bytes=VMEM_LIMIT)


def on_device(devices, chans, query_in, key_in, value_in, short_taps, long_filter, skip_gain, w_out):
    width = query_in.shape[1]
    rows = width // LANES
    per = rows // devices
    near = chans // 2
    forward_first, turn, forward_second, inverse_second, inverse_first, basis = tables(rows, devices)
    message_shape = (devices, 4 * per // PACK + 1, PACK, LANES)
    message, skipped = pl.pallas_call(
        functools.partial(forward_kernel, devices),
        in_specs=[HBM] * 8,
        out_specs=[HBM, VMEM],
        out_shape=[jax.ShapeDtypeStruct(message_shape, BF16), jax.ShapeDtypeStruct((rows, LANES), F32)],
        scratch_shapes=[
            pltpu.VMEM(short_taps.shape, F32),
            pltpu.VMEM((1, width), BF16),
            pltpu.VMEM((1, width), BF16),
            pltpu.VMEM((2, 1, LANES), BF16),
            pltpu.VMEM((rows, LANES), F32),
            pltpu.VMEM(forward_first.shape, BF16),
            pltpu.VMEM(turn.shape, F32),
            pltpu.VMEM(forward_second.shape, BF16),
            pltpu.SemaphoreType.DMA((9,)),
            pltpu.VMEM(message_shape, BF16),
            pltpu.SemaphoreType.DMA((CHUNKS,)),
        ],
        compiler_params=PARAMS,
        name="forward",
    )(
        *(
            pltpu.with_memory_space_constraint(jnp.asarray(operand), pltpu.HBM)
            for operand in (
                short_taps, key_in, value_in, query_in, long_filter.reshape(rows, LANES),
                forward_first, turn, forward_second,
            )
        ),
    )
    q_feat, scalars = pl.pallas_call(
        functools.partial(side_kernel, devices),
        in_specs=[VMEM] * 3,
        out_specs=[VMEM] * 2,
        out_shape=[jax.ShapeDtypeStruct((rows, LANES), BF16), jax.ShapeDtypeStruct((8 + 2 * chans, LANES), F32)],
        compiler_params=PARAMS,
        cost_estimate=pl.CostEstimate(flops=400_000, bytes_accessed=400_000, transcendentals=0),
        name="side",
    )(short_taps, query_in, w_out)
    message = lax.all_to_all(message, "seq", 0, 0)
    spectra, heads = pl.pallas_call(
        functools.partial(middle_kernel, devices),
        in_specs=[SMEM] + [VMEM] * 3,
        out_specs=[VMEM] * 2,
        out_shape=[
            jax.ShapeDtypeStruct((devices, 2 * per, LANES), BF16),
            jax.ShapeDtypeStruct((8, LANES), F32),
        ],
        scratch_shapes=[pltpu.VMEM((2, devices, LANES), F32)] * 2 + [pltpu.VMEM((devices, 4 * per, LANES), F32)],
        compiler_params=PARAMS,
        name="middle",
    )(skip_gain, scalars, message.reshape(-1, LANES), basis)
    spectra = lax.all_to_all(spectra, "seq", 0, 0)
    gating = pl.pallas_call(
        functools.partial(inverse_kernel, devices),
        in_specs=[VMEM] * 7,
        out_specs=VMEM,
        out_shape=jax.ShapeDtypeStruct((rows, LANES), BF16),
        compiler_params=PARAMS,
        name="inverse",
    )(spectra, turn, inverse_second, inverse_first, q_feat, skipped, heads)
    gathered = [gating] + [
        lax.ppermute(gating, "chan", [(c, c // near * near + (c + step) % near) for c in range(chans)])
        for step in range(1, near)
    ]
    own, other = pl.pallas_call(
        mix_kernel,
        in_specs=[VMEM] * (near + 1),
        out_specs=[VMEM] * 2,
        out_shape=[jax.ShapeDtypeStruct((rows, LANES), F32), jax.ShapeDtypeStruct((rows, LANES), BF16)],
        compiler_params=PARAMS,
        name="mix",
    )(scalars, *gathered)
    other = lax.ppermute(other, "chan", [(c, (c + near) % chans) for c in range(chans)])
    return pl.pallas_call(
        add_kernel,
        in_specs=[VMEM] * 2,
        out_specs=VMEM,
        out_shape=jax.ShapeDtypeStruct((1, width), BF16),
        compiler_params=PARAMS,
        name="add",
    )(own, other)


def solution(mesh):
    return jax.shard_map(
        functools.partial(on_device, mesh.shape["seq"], mesh.shape["chan"]),
        mesh=mesh,
        in_specs=(
            P("chan", "seq"),
            P("chan", "seq"),
            P("chan", "seq"),
            P(None, "chan", None),
            P("chan", "seq"),
            P("chan"),
            P(),
        ),
        out_specs=P("chan", "seq"),
        check_vma=False,
    )
```

```python
import functools
import math

import jax
import jax.numpy as jnp
import ml_dtypes
import numpy as np
from jax import lax
from jax.experimental import pallas as pl
from jax.experimental.pallas import tpu as pltpu
from jax.sharding import PartitionSpec as P

LANES = 128
PACK = 2
CHUNKS = 2
F32 = jnp.float32
BF16 = jnp.bfloat16
VMEM_LIMIT = 40 * 1024 * 1024


def tables(rows, devices):
    length = rows * LANES
    per = rows // devices
    k1 = np.arange(rows)
    first = 2.0 * math.pi * np.outer(k1 + 0.25, np.arange(rows)) / rows
    forward_first = np.stack([np.cos(first), -np.sin(first)])
    forward_first = forward_first.reshape(2, devices, per, rows).transpose(1, 0, 2, 3).reshape(2 * rows, rows)
    inverse_first = np.concatenate([np.cos(first), -np.sin(first)]).T / length
    turn = 2.0 * math.pi * np.outer(k1 + 0.25, np.arange(LANES)) / length
    turn = np.stack([np.cos(turn), np.sin(turn)])
    second = 2.0 * math.pi * np.outer(np.arange(LANES), np.arange(LANES)) / LANES
    cos, sin = np.cos(second), np.sin(second)
    forward_second = np.block([[cos, -sin], [sin, cos]])
    inverse_second = np.block([[cos, sin], [-sin, cos]])
    basis = 2.0 * math.pi * (np.arange(per)[:, None] + 0.25 + rows * np.arange(LANES)[None, :]) / length
    basis = np.stack([np.cos(basis), -np.sin(basis)])
    half = lambda values: values.astype(ml_dtypes.bfloat16)
    return (
        half(forward_first),
        turn.astype(np.float32),
        half(forward_second),
        half(inverse_second),
        half(inverse_first),
        basis.astype(np.float32),
    )


def members(devices):
    if devices != 32:
        return list(range(devices))
    middle = (2, 1, 3, 0)
    return [x * 8 + z * 2 + core for z in middle for x in middle for core in (1, 0)]


def dot(left, right):
    return jnp.dot(left, right, preferred_element_type=F32)


def moved_on(values, lane, row):
    turned = pltpu.roll(values, 1, 1)
    carried = jnp.where(row == 0, 0.0, pltpu.roll(turned, 1, 0))
    return jnp.where(lane == 0, carried, turned)


def featurized(signal, taps, stream):
    lane = lax.broadcasted_iota(jnp.int32, signal.shape, 1)
    row = lax.broadcasted_iota(jnp.int32, signal.shape, 0)
    once = moved_on(signal, lane, row)
    twice = moved_on(once, lane, row)
    summed = taps[stream][0] * signal + taps[stream][1] * once + taps[stream][2] * twice
    return summed.astype(BF16)


def at_lanes(values, first):
    return pltpu.roll(values, first, 1) if first else values


def forward_kernel(devices, taps_hbm, k_hbm, v_hbm, q_hbm, filter_hbm, first_hbm, turn_hbm, second_hbm,
                   message_hbm, product_ref,
                   taps_ref, k_ref, v_ref, q_ref, filter_ref, first_ref, turn_ref, second_ref, sems, message_ref, out_sems):
    width = k_hbm.shape[1]
    pairs = (
        (taps_hbm, taps_ref),
        (k_hbm, k_ref),
        (v_hbm, v_ref),
        (filter_hbm, filter_ref),
        (first_hbm, first_ref),
        (q_hbm.at[:, pl.ds(0, LANES)], q_ref.at[0]),
        (q_hbm.at[:, pl.ds(width - LANES, LANES)], q_ref.at[1]),
        (turn_hbm, turn_ref),
        (second_hbm, second_ref),
    )
    copies = [pltpu.make_async_copy(source, target, sems.at[i]) for i, (source, target) in enumerate(pairs)]
    for copy in copies:
        copy.start()
    rows = product_ref.shape[0]
    per = rows // devices
    lane = lax.broadcasted_iota(jnp.int32, (1, LANES), 1)
    copies[0].wait()
    taps = [[taps_ref[stream, :, j : j + 1] for j in range(3)] for stream in range(3)]
    for copy in copies[1:]:
        copy.wait()
    key = k_ref[...].astype(F32).reshape(rows, LANES)
    k_feat = featurized(key, taps, 1)
    value = v_ref[...].astype(F32).reshape(rows, LANES)
    v_feat = featurized(value, taps, 2)
    product = k_feat.astype(F32) * v_feat.astype(F32)
    product_ref[...] = product
    signals = jnp.concatenate([product, filter_ref[...]], axis=1).astype(BF16)
    values = dot(first_ref[...], signals).reshape(devices, 2, per, 2 * LANES)
    edges = jnp.zeros((1, LANES), F32)
    pieces = ((key[:1], key[rows - 1 :]), (value[:1], value[rows - 1 :]), (q_ref[0].astype(F32), q_ref[1].astype(F32)))
    for i, (head, tail) in enumerate(pieces):
        ends = jnp.where(lane < 2, head, jnp.where(lane < LANES - 2, 0.0, tail))
        edges = edges + at_lanes(ends, 4 * i)
    row = lax.broadcasted_iota(jnp.int32, (8, LANES), 0)
    edges = jnp.where(row == 0, jnp.broadcast_to(edges, (8, LANES)), 0.0)[:PACK].astype(BF16)
    packs = 4 * per // PACK
    count = devices // CHUNKS
    for chunk in range(CHUNKS):
        part = slice(chunk * count, (chunk + 1) * count)
        lines = slice(chunk * count * per, (chunk + 1) * count * per)
        real, imag = values[part, 0], values[part, 1]
        turn_real = turn_ref[0, lines].reshape(count, per, LANES)
        turn_imag = turn_ref[1, lines].reshape(count, per, LANES)
        packed = []
        for signal in range(2):
            lanes = slice(signal * LANES, (signal + 1) * LANES)
            a, b = real[:, :, lanes], imag[:, :, lanes]
            packed.append(
                jnp.concatenate([a * turn_real + b * turn_imag, b * turn_real - a * turn_imag], axis=2)
            )
        packed = jnp.concatenate(packed, axis=1).reshape(2 * count * per, 2 * LANES).astype(BF16)
        spectra = dot(packed, second_ref[...]).reshape(count, 2 * per, 2 * LANES)
        spectra = jnp.concatenate(
            [
                spectra[:, :per, :LANES],
                spectra[:, :per, LANES:],
                spectra[:, per:, :LANES],
                spectra[:, per:, LANES:],
            ],
            axis=1,
        ).astype(BF16)
        message_ref[part, :packs] = spectra.reshape(count, packs, PACK, LANES)
        message_ref[part, packs] = jnp.broadcast_to(edges[None], (count, PACK, LANES))
        copies.append(pltpu.make_async_copy(message_ref.at[part], message_hbm.at[part], out_sems.at[chunk]))
        copies[-1].start()
    for copy in copies[9:]:
        copy.wait()


def side_kernel(devices, taps_ref, q_ref, w_ref, q_feat_ref, scalars_ref):
    rows = q_feat_ref.shape[0]
    own_chan = lax.axis_index("chan")
    lane = lax.broadcasted_iota(jnp.int32, (1, LANES), 1)
    taps = [[taps_ref[stream, :, j : j + 1] for j in range(3)] for stream in range(3)]
    for j in range(3):
        scalars_ref[j : j + 1, :] = jnp.where(lane < 4, taps[1][j], jnp.where(lane < 8, taps[2][j], taps[0][j]))
    query = q_ref[...].astype(F32).reshape(rows, LANES)
    q_feat_ref[...] = featurized(query, taps, 0)
    chans = w_ref.shape[0]
    weights = w_ref[...].astype(F32)
    column = lax.broadcasted_iota(jnp.int32, weights.shape, 1)
    for i, chan in enumerate((own_chan, (own_chan + chans // 2) % chans)):
        picked = jnp.sum(jnp.where(column == chan, weights, 0.0), axis=1, keepdims=True)
        scalars_ref[8 + i * chans : 8 + (i + 1) * chans, :] = jnp.broadcast_to(picked, (chans, LANES))


def rounded(values):
    return values.astype(BF16).astype(F32)


def middle_kernel(devices, skip_ref, scalars_ref, message_ref, basis_ref, out_ref, heads_ref, heads_scratch, error_scratch, aligned_ref):
    pitch = message_ref.shape[0] // devices
    per = (pitch - PACK) // 4
    message = message_ref[...].astype(F32)
    own = lax.axis_index("seq")
    order = members(devices)
    own_slice = sum(jnp.where(own == device, i, 0) for i, device in enumerate(order))
    slabs = [order.index(p) * pitch for p in range(devices)]
    edges = jnp.concatenate([message[slab + 4 * per : slab + 4 * per + 1] for slab in slabs], axis=0)
    before = jnp.concatenate([jnp.zeros((1, LANES), F32), edges[:-1]], axis=0)
    lane = lax.broadcasted_iota(jnp.int32, edges.shape, 1)
    taps = [scalars_ref[j : j + 1, :] for j in range(3)]
    once = pltpu.roll(edges, 1, 1)
    alone = taps[0] * edges + taps[1] * jnp.where(lane % 4 == 0, 0.0, once)
    once = jnp.where(lane % 4 == 0, pltpu.roll(before, 1, 1), once)
    heads = rounded(taps[0] * edges + taps[1] * once + taps[2] * pltpu.roll(before, 2, 1))
    alone = rounded(alone)
    product = heads * pltpu.roll(heads, LANES - 4, 1)
    error = product - alone * pltpu.roll(alone, LANES - 4, 1)
    error = jnp.where(lax.broadcasted_iota(jnp.int32, edges.shape, 0) == 0, 0.0, error)
    for i in range(2):
        error_scratch[i] = jnp.broadcast_to(error[:, i : i + 1], edges.shape)
    heads_scratch[0] = pltpu.roll(heads, LANES - 8, 1)
    heads_scratch[1] = product
    for i in range(2):
        heads_ref[i : i + 1, :] = heads_scratch[i, pl.ds(own, 1), :]
    heads_ref[2:3, :] = jnp.full((1, LANES), skip_ref[0], F32)
    angle = jnp.full((per, LANES), own_slice, jnp.int32).astype(F32) * (2.0 * math.pi / (devices * LANES))
    square = angle * angle
    cos = 1.0 - square * (0.5 - square * (1.0 / 24.0))
    sin = angle * (1.0 - square * (1.0 / 6.0 - square * (1.0 / 120.0)))
    basis_real, basis_imag = basis_ref[0], basis_ref[1]
    point_real = basis_real * cos + basis_imag * sin
    point_imag = basis_imag * cos - basis_real * sin
    blocks = []
    for p in range(devices):
        aligned_ref[p] = message[slabs[p] : slabs[p] + 4 * per]
    for p in range(devices):
        block = aligned_ref[p]
        real, imag = block[:per], block[per : 2 * per]
        if p > 0:
            first = error_scratch[1, p : p + 1, :]
            real = real + (error_scratch[0, p : p + 1, :] + first * point_real)
            imag = imag + first * point_imag
        c, d = block[2 * per : 3 * per], block[3 * per : 4 * per]
        blocks.append((real + imag, real, imag, c, d - c, c + d))
    behind_real = jnp.zeros((per, LANES), F32)
    behind_imag = behind_real
    for p in range(devices):
        sums = [None] * 3
        for q in range(p + 1):
            for i in range(3):
                term = blocks[q][i] * blocks[p - q][3 + i]
                sums[i] = term if sums[i] is None else sums[i] + term
        real, imag = sums[0] - sums[2], sums[0] + sums[1]
        out_ref[order.index(p)] = jnp.concatenate([real - behind_imag, imag + behind_real], axis=0).astype(BF16)
        behind_real, behind_imag = real, imag


def inverse_kernel(devices, spectra_ref, turn_ref, second_ref, first_ref, q_feat_ref, skipped_ref, heads_ref, gating_ref):
    rows = q_feat_ref.shape[0]
    per = rows // devices
    packed = jnp.concatenate(
        [spectra_ref[:, :per, :].astype(F32), spectra_ref[:, per:, :].astype(F32)], axis=2
    )
    values = dot(packed.reshape(rows, 2 * LANES).astype(BF16), second_ref[...])
    a, b = values[:, :LANES], values[:, LANES:]
    turn_real, turn_imag = turn_ref[0], turn_ref[1]
    turned = jnp.concatenate([a * turn_real - b * turn_imag, a * turn_imag + b * turn_real], axis=0)
    convolved = dot(first_ref[...], turned.astype(BF16))
    lane = lax.broadcasted_iota(jnp.int32, (rows, LANES), 1)
    row = lax.broadcasted_iota(jnp.int32, (rows, LANES), 0)
    head = (row == 0) & (lane < 2)
    q_feat = jnp.where(head, heads_ref[0:1, :], q_feat_ref[...].astype(F32))
    skipped = heads_ref[2:3, :] * jnp.where(head, heads_ref[1:2, :], skipped_ref[...])
    gating = (q_feat * (convolved + skipped)).astype(BF16)
    gating_ref[...] = gating


def mix_kernel(scalars_ref, *refs):
    *gating_refs, own_ref, other_ref = refs
    near = len(gating_refs)
    chans = 2 * near
    own_chan = lax.axis_index("chan")
    start = 8 + own_chan // near * near
    own = other = None
    for step, gating_ref in enumerate(gating_refs):
        gating = gating_ref[...].astype(F32)
        row = start + (own_chan + near - step) % near
        to_own = scalars_ref[pl.ds(row, 1), :] * gating
        to_other = scalars_ref[pl.ds(row + chans, 1), :] * gating
        own = to_own if own is None else own + to_own
        other = to_other if other is None else other + to_other
    own_ref[...] = own
    other_ref[...] = other.astype(BF16)


def add_kernel(own_ref, other_ref, out_ref):
    out_ref[...] = (own_ref[...] + other_ref[...].astype(F32)).reshape(out_ref.shape).astype(BF16)


SMEM = pl.BlockSpec(memory_space=pltpu.SMEM)
VMEM = pl.BlockSpec(memory_space=pltpu.VMEM)
HBM = pl.BlockSpec(memory_space=pltpu.HBM)
PARAMS = pltpu.CompilerParams(vmem_limit_bytes=VMEM_LIMIT)


def on_device(devices, chans, query_in, key_in, value_in, short_taps, long_filter, skip_gain, w_out):
    width = query_in.shape[1]
    rows = width // LANES
    per = rows // devices
    near = chans // 2
    forward_first, turn, forward_second, inverse_second, inverse_first, basis = tables(rows, devices)
    message_shape = (devices, 4 * per // PACK + 1, PACK, LANES)
    message, skipped = pl.pallas_call(
        functools.partial(forward_kernel, devices),
        in_specs=[HBM] * 8,
        out_specs=[HBM, VMEM],
        out_shape=[jax.ShapeDtypeStruct(message_shape, BF16), jax.ShapeDtypeStruct((rows, LANES), F32)],
        scratch_shapes=[
            pltpu.VMEM(short_taps.shape, F32),
            pltpu.VMEM((1, width), BF16),
            pltpu.VMEM((1, width), BF16),
            pltpu.VMEM((2, 1, LANES), BF16),
            pltpu.VMEM((rows, LANES), F32),
            pltpu.VMEM(forward_first.shape, BF16),
            pltpu.VMEM(turn.shape, F32),
            pltpu.VMEM(forward_second.shape, BF16),
            pltpu.SemaphoreType.DMA((9,)),
            pltpu.VMEM(message_shape, BF16),
            pltpu.SemaphoreType.DMA((CHUNKS,)),
        ],
        compiler_params=PARAMS,
        name="forward",
    )(
        *(
            pltpu.with_memory_space_constraint(jnp.asarray(operand), pltpu.HBM)
            for operand in (
                short_taps, key_in, value_in, query_in, long_filter.reshape(rows, LANES),
                forward_first, turn, forward_second,
            )
        ),
    )
    q_feat, scalars = pl.pallas_call(
        functools.partial(side_kernel, devices),
        in_specs=[VMEM] * 3,
        out_specs=[VMEM] * 2,
        out_shape=[jax.ShapeDtypeStruct((rows, LANES), BF16), jax.ShapeDtypeStruct((8 + 2 * chans, LANES), F32)],
        compiler_params=PARAMS,
        cost_estimate=pl.CostEstimate(flops=400_000, bytes_accessed=400_000, transcendentals=0),
        name="side",
    )(short_taps, query_in, w_out)
    group = [members(devices)]
    message = lax.all_to_all(message, "seq", 0, 0, axis_index_groups=group)
    spectra, heads = pl.pallas_call(
        functools.partial(middle_kernel, devices),
        in_specs=[SMEM] + [VMEM] * 3,
        out_specs=[VMEM] * 2,
        out_shape=[
            jax.ShapeDtypeStruct((devices, 2 * per, LANES), BF16),
            jax.ShapeDtypeStruct((8, LANES), F32),
        ],
        scratch_shapes=[pltpu.VMEM((2, devices, LANES), F32)] * 2 + [pltpu.VMEM((devices, 4 * per, LANES), F32)],
        compiler_params=PARAMS,
        name="middle",
    )(skip_gain, scalars, message.reshape(-1, LANES), basis)
    spectra = lax.all_to_all(spectra, "seq", 0, 0, axis_index_groups=group)
    gating = pl.pallas_call(
        functools.partial(inverse_kernel, devices),
        in_specs=[VMEM] * 7,
        out_specs=VMEM,
        out_shape=jax.ShapeDtypeStruct((rows, LANES), BF16),
        compiler_params=PARAMS,
        name="inverse",
    )(spectra, turn, inverse_second, inverse_first, q_feat, skipped, heads)
    gathered = [gating] + [
        lax.ppermute(gating, "chan", [(c, c // near * near + (c + step) % near) for c in range(chans)])
        for step in range(1, near)
    ]
    own, other = pl.pallas_call(
        mix_kernel,
        in_specs=[VMEM] * (near + 1),
        out_specs=[VMEM] * 2,
        out_shape=[jax.ShapeDtypeStruct((rows, LANES), F32), jax.ShapeDtypeStruct((rows, LANES), BF16)],
        compiler_params=PARAMS,
        name="mix",
    )(scalars, *gathered)
    other = lax.ppermute(other, "chan", [(c, (c + near) % chans) for c in range(chans)])
    return pl.pallas_call(
        add_kernel,
        in_specs=[VMEM] * 2,
        out_specs=VMEM,
        out_shape=jax.ShapeDtypeStruct((1, width), BF16),
        compiler_params=PARAMS,
        name="add",
    )(own, other)


def solution(mesh):
    return jax.shard_map(
        functools.partial(on_device, mesh.shape["seq"], mesh.shape["chan"]),
        mesh=mesh,
        in_specs=(
            P("chan", "seq"),
            P("chan", "seq"),
            P("chan", "seq"),
            P(None, "chan", None),
            P("chan", "seq"),
            P("chan"),
            P(),
        ),
        out_specs=P("chan", "seq"),
        check_vma=False,
    )
```

```python
import functools
import math

import jax
import jax.numpy as jnp
import ml_dtypes
import numpy as np
from jax import lax
from jax.experimental import pallas as pl
from jax.experimental.pallas import tpu as pltpu
from jax.sharding import PartitionSpec as P

LANES = 128
PACK = 2
CHUNKS = 2
F32 = jnp.float32
BF16 = jnp.bfloat16
VMEM_LIMIT = 40 * 1024 * 1024


def tables(rows, devices):
    length = rows * LANES
    per = rows // devices
    k1 = np.arange(rows)
    first = 2.0 * math.pi * np.outer(k1 + 0.25, np.arange(rows)) / rows
    forward_first = np.stack([np.cos(first), -np.sin(first)])
    forward_first = forward_first.reshape(2, devices, per, rows).transpose(1, 0, 2, 3).reshape(2 * rows, rows)
    inverse_first = np.concatenate([np.cos(first), -np.sin(first)]).T / length
    turn = 2.0 * math.pi * np.outer(k1 + 0.25, np.arange(LANES)) / length
    turn = np.stack([np.cos(turn), np.sin(turn)])
    second = 2.0 * math.pi * np.outer(np.arange(LANES), np.arange(LANES)) / LANES
    cos, sin = np.cos(second), np.sin(second)
    forward_second = np.block([[cos, -sin], [sin, cos]])
    inverse_second = np.block([[cos, sin], [-sin, cos]])
    basis = 2.0 * math.pi * (np.arange(per)[:, None] + 0.25 + rows * np.arange(LANES)[None, :]) / length
    basis = np.stack([np.cos(basis), -np.sin(basis)])
    half = lambda values: values.astype(ml_dtypes.bfloat16)
    return (
        half(forward_first),
        turn.astype(np.float32),
        half(forward_second),
        half(inverse_second),
        half(inverse_first),
        basis.astype(np.float32),
    )


def members(devices):
    if devices != 32:
        return list(range(devices))
    return [x * 8 + z * 2 + core for z in (2, 3, 1, 0) for x in (2, 3, 1, 0) for core in (1, 0)]


def dot(left, right):
    return jnp.dot(left, right, preferred_element_type=F32)


def moved_on(values, lane, row):
    turned = pltpu.roll(values, 1, 1)
    carried = jnp.where(row == 0, 0.0, pltpu.roll(turned, 1, 0))
    return jnp.where(lane == 0, carried, turned)


def featurized(signal, taps, stream):
    lane = lax.broadcasted_iota(jnp.int32, signal.shape, 1)
    row = lax.broadcasted_iota(jnp.int32, signal.shape, 0)
    once = moved_on(signal, lane, row)
    twice = moved_on(once, lane, row)
    summed = taps[stream][0] * signal + taps[stream][1] * once + taps[stream][2] * twice
    return summed.astype(BF16)


def at_lanes(values, first):
    return pltpu.roll(values, first, 1) if first else values


def forward_kernel(devices, taps_hbm, k_hbm, v_hbm, q_hbm, filter_hbm, first_hbm, turn_hbm, second_hbm,
                   message_hbm, product_ref,
                   taps_ref, k_ref, v_ref, q_ref, filter_ref, first_ref, turn_ref, second_ref, sems, message_ref, out_sems):
    width = k_hbm.shape[1]
    pairs = (
        (taps_hbm, taps_ref),
        (k_hbm, k_ref),
        (v_hbm, v_ref),
        (filter_hbm, filter_ref),
        (first_hbm, first_ref),
        (q_hbm.at[:, pl.ds(0, LANES)], q_ref.at[0]),
        (q_hbm.at[:, pl.ds(width - LANES, LANES)], q_ref.at[1]),
        (turn_hbm, turn_ref),
        (second_hbm, second_ref),
    )
    copies = [pltpu.make_async_copy(source, target, sems.at[i]) for i, (source, target) in enumerate(pairs)]
    for copy in copies:
        copy.start()
    rows = product_ref.shape[0]
    per = rows // devices
    lane = lax.broadcasted_iota(jnp.int32, (1, LANES), 1)
    copies[0].wait()
    taps = [[taps_ref[stream, :, j : j + 1] for j in range(3)] for stream in range(3)]
    for copy in copies[1:3]:
        copy.wait()
    key = k_ref[...].astype(F32).reshape(rows, LANES)
    k_feat = featurized(key, taps, 1)
    value = v_ref[...].astype(F32).reshape(rows, LANES)
    v_feat = featurized(value, taps, 2)
    product = k_feat.astype(F32) * v_feat.astype(F32)
    product_ref[...] = product
    for copy in copies[3:]:
        copy.wait()
    signals = jnp.concatenate([product, filter_ref[...]], axis=1).astype(BF16)
    values = dot(first_ref[...], signals).reshape(devices, 2, per, 2 * LANES)
    edges = jnp.zeros((1, LANES), F32)
    pieces = ((key[:1], key[rows - 1 :]), (value[:1], value[rows - 1 :]), (q_ref[0].astype(F32), q_ref[1].astype(F32)))
    for i, (head, tail) in enumerate(pieces):
        ends = jnp.where(lane < 2, head, jnp.where(lane < LANES - 2, 0.0, tail))
        edges = edges + at_lanes(ends, 4 * i)
    row = lax.broadcasted_iota(jnp.int32, (8, LANES), 0)
    edges = jnp.where(row == 0, jnp.broadcast_to(edges, (8, LANES)), 0.0)[:PACK].astype(BF16)
    packs = 4 * per // PACK
    count = devices // CHUNKS
    for chunk in range(CHUNKS):
        part = slice(chunk * count, (chunk + 1) * count)
        lines = slice(chunk * count * per, (chunk + 1) * count * per)
        real, imag = values[part, 0], values[part, 1]
        turn_real = turn_ref[0, lines].reshape(count, per, LANES)
        turn_imag = turn_ref[1, lines].reshape(count, per, LANES)
        packed = []
        for signal in range(2):
            lanes = slice(signal * LANES, (signal + 1) * LANES)
            a, b = real[:, :, lanes], imag[:, :, lanes]
            packed.append(
                jnp.concatenate([a * turn_real + b * turn_imag, b * turn_real - a * turn_imag], axis=2)
            )
        packed = jnp.concatenate(packed, axis=1).reshape(2 * count * per, 2 * LANES).astype(BF16)
        spectra = dot(packed, second_ref[...]).reshape(count, 2 * per, 2 * LANES)
        spectra = jnp.concatenate(
            [
                spectra[:, :per, :LANES],
                spectra[:, :per, LANES:],
                spectra[:, per:, :LANES],
                spectra[:, per:, LANES:],
            ],
            axis=1,
        ).astype(BF16)
        message_ref[part, :packs] = spectra.reshape(count, packs, PACK, LANES)
        message_ref[part, packs] = jnp.broadcast_to(edges[None], (count, PACK, LANES))
        copies.append(pltpu.make_async_copy(message_ref.at[part], message_hbm.at[part], out_sems.at[chunk]))
        copies[-1].start()
    for copy in copies[9:]:
        copy.wait()


def side_kernel(devices, taps_ref, q_ref, w_ref, q_feat_ref, scalars_ref):
    rows = q_feat_ref.shape[0]
    own_chan = lax.axis_index("chan")
    lane = lax.broadcasted_iota(jnp.int32, (1, LANES), 1)
    taps = [[taps_ref[stream, :, j : j + 1] for j in range(3)] for stream in range(3)]
    for j in range(3):
        scalars_ref[j : j + 1, :] = jnp.where(lane < 4, taps[1][j], jnp.where(lane < 8, taps[2][j], taps[0][j]))
    query = q_ref[...].astype(F32).reshape(rows, LANES)
    q_feat_ref[...] = featurized(query, taps, 0)
    chans = w_ref.shape[0]
    weights = w_ref[...].astype(F32)
    column = lax.broadcasted_iota(jnp.int32, weights.shape, 1)
    for i, chan in enumerate((own_chan, (own_chan + chans // 2) % chans)):
        picked = jnp.sum(jnp.where(column == chan, weights, 0.0), axis=1, keepdims=True)
        scalars_ref[8 + i * chans : 8 + (i + 1) * chans, :] = jnp.broadcast_to(picked, (chans, LANES))


def rounded(values):
    return values.astype(BF16).astype(F32)


def middle_kernel(devices, skip_ref, scalars_ref, message_ref, basis_ref, out_ref, heads_ref, heads_scratch, error_scratch, aligned_ref):
    pitch = message_ref.shape[0] // devices
    per = (pitch - PACK) // 4
    message = message_ref[...].astype(F32)
    own = lax.axis_index("seq")
    order = members(devices)
    own_slice = sum(jnp.where(own == device, i, 0) for i, device in enumerate(order))
    slabs = [order.index(p) * pitch for p in range(devices)]
    edges = jnp.concatenate([message[slab + 4 * per : slab + 4 * per + 1] for slab in slabs], axis=0)
    before = jnp.concatenate([jnp.zeros((1, LANES), F32), edges[:-1]], axis=0)
    lane = lax.broadcasted_iota(jnp.int32, edges.shape, 1)
    taps = [scalars_ref[j : j + 1, :] for j in range(3)]
    once = pltpu.roll(edges, 1, 1)
    alone = taps[0] * edges + taps[1] * jnp.where(lane % 4 == 0, 0.0, once)
    once = jnp.where(lane % 4 == 0, pltpu.roll(before, 1, 1), once)
    heads = rounded(taps[0] * edges + taps[1] * once + taps[2] * pltpu.roll(before, 2, 1))
    alone = rounded(alone)
    product = heads * pltpu.roll(heads, LANES - 4, 1)
    error = product - alone * pltpu.roll(alone, LANES - 4, 1)
    error = jnp.where(lax.broadcasted_iota(jnp.int32, edges.shape, 0) == 0, 0.0, error)
    for i in range(2):
        error_scratch[i] = jnp.broadcast_to(error[:, i : i + 1], edges.shape)
    heads_scratch[0] = pltpu.roll(heads, LANES - 8, 1)
    heads_scratch[1] = product
    for i in range(2):
        heads_ref[i : i + 1, :] = heads_scratch[i, pl.ds(own, 1), :]
    heads_ref[2:3, :] = jnp.full((1, LANES), skip_ref[0], F32)
    angle = jnp.full((per, LANES), own_slice, jnp.int32).astype(F32) * (2.0 * math.pi / (devices * LANES))
    square = angle * angle
    cos = 1.0 - square * (0.5 - square * (1.0 / 24.0))
    sin = angle * (1.0 - square * (1.0 / 6.0 - square * (1.0 / 120.0)))
    basis_real, basis_imag = basis_ref[0], basis_ref[1]
    point_real = basis_real * cos + basis_imag * sin
    point_imag = basis_imag * cos - basis_real * sin
    blocks = []
    for p in range(devices):
        aligned_ref[p] = message[slabs[p] : slabs[p] + 4 * per]
    for p in range(devices):
        block = aligned_ref[p]
        real, imag = block[:per], block[per : 2 * per]
        if p > 0:
            first = error_scratch[1, p : p + 1, :]
            real = real + (error_scratch[0, p : p + 1, :] + first * point_real)
            imag = imag + first * point_imag
        c, d = block[2 * per : 3 * per], block[3 * per : 4 * per]
        blocks.append((real + imag, real, imag, c, d - c, c + d))
    behind_real = jnp.zeros((per, LANES), F32)
    behind_imag = behind_real
    for p in range(devices):
        sums = [None] * 3
        for q in range(p + 1):
            for i in range(3):
                term = blocks[q][i] * blocks[p - q][3 + i]
                sums[i] = term if sums[i] is None else sums[i] + term
        real, imag = sums[0] - sums[2], sums[0] + sums[1]
        out_ref[order.index(p)] = jnp.concatenate([real - behind_imag, imag + behind_real], axis=0).astype(BF16)
        behind_real, behind_imag = real, imag


def inverse_kernel(devices, spectra_ref, turn_ref, second_ref, first_ref, q_feat_ref, skipped_ref, heads_ref, gating_ref):
    rows = q_feat_ref.shape[0]
    per = rows // devices
    packed = jnp.concatenate(
        [spectra_ref[:, :per, :].astype(F32), spectra_ref[:, per:, :].astype(F32)], axis=2
    )
    values = dot(packed.reshape(rows, 2 * LANES).astype(BF16), second_ref[...])
    a, b = values[:, :LANES], values[:, LANES:]
    turn_real, turn_imag = turn_ref[0], turn_ref[1]
    turned = jnp.concatenate([a * turn_real - b * turn_imag, a * turn_imag + b * turn_real], axis=0)
    convolved = dot(first_ref[...], turned.astype(BF16))
    lane = lax.broadcasted_iota(jnp.int32, (rows, LANES), 1)
    row = lax.broadcasted_iota(jnp.int32, (rows, LANES), 0)
    head = (row == 0) & (lane < 2)
    q_feat = jnp.where(head, heads_ref[0:1, :], q_feat_ref[...].astype(F32))
    skipped = heads_ref[2:3, :] * jnp.where(head, heads_ref[1:2, :], skipped_ref[...])
    gating = (q_feat * (convolved + skipped)).astype(BF16)
    gating_ref[...] = gating


def mix_kernel(scalars_ref, *refs):
    *gating_refs, own_ref, other_ref = refs
    near = len(gating_refs)
    chans = 2 * near
    own_chan = lax.axis_index("chan")
    start = 8 + own_chan // near * near
    own = other = None
    for step, gating_ref in enumerate(gating_refs):
        gating = gating_ref[...].astype(F32)
        row = start + (own_chan + near - step) % near
        to_own = scalars_ref[pl.ds(row, 1), :] * gating
        to_other = scalars_ref[pl.ds(row + chans, 1), :] * gating
        own = to_own if own is None else own + to_own
        other = to_other if other is None else other + to_other
    own_ref[...] = own
    other_ref[...] = other.astype(BF16)


def add_kernel(own_ref, other_ref, out_ref):
    out_ref[...] = (own_ref[...] + other_ref[...].astype(F32)).reshape(out_ref.shape).astype(BF16)


SMEM = pl.BlockSpec(memory_space=pltpu.SMEM)
VMEM = pl.BlockSpec(memory_space=pltpu.VMEM)
HBM = pl.BlockSpec(memory_space=pltpu.HBM)
PARAMS = pltpu.CompilerParams(vmem_limit_bytes=VMEM_LIMIT)


def on_device(devices, chans, query_in, key_in, value_in, short_taps, long_filter, skip_gain, w_out):
    width = query_in.shape[1]
    rows = width // LANES
    per = rows // devices
    near = chans // 2
    forward_first, turn, forward_second, inverse_second, inverse_first, basis = tables(rows, devices)
    message_shape = (devices, 4 * per // PACK + 1, PACK, LANES)
    message, skipped = pl.pallas_call(
        functools.partial(forward_kernel, devices),
        in_specs=[HBM] * 8,
        out_specs=[HBM, VMEM],
        out_shape=[jax.ShapeDtypeStruct(message_shape, BF16), jax.ShapeDtypeStruct((rows, LANES), F32)],
        scratch_shapes=[
            pltpu.VMEM(short_taps.shape, F32),
            pltpu.VMEM((1, width), BF16),
            pltpu.VMEM((1, width), BF16),
            pltpu.VMEM((2, 1, LANES), BF16),
            pltpu.VMEM((rows, LANES), F32),
            pltpu.VMEM(forward_first.shape, BF16),
            pltpu.VMEM(turn.shape, F32),
            pltpu.VMEM(forward_second.shape, BF16),
            pltpu.SemaphoreType.DMA((9,)),
            pltpu.VMEM(message_shape, BF16),
            pltpu.SemaphoreType.DMA((CHUNKS,)),
        ],
        compiler_params=PARAMS,
        name="forward",
    )(
        *(
            pltpu.with_memory_space_constraint(jnp.asarray(operand), pltpu.HBM)
            for operand in (
                short_taps, key_in, value_in, query_in, long_filter.reshape(rows, LANES),
                forward_first, turn, forward_second,
            )
        ),
    )
    q_feat, scalars = pl.pallas_call(
        functools.partial(side_kernel, devices),
        in_specs=[VMEM] * 3,
        out_specs=[VMEM] * 2,
        out_shape=[jax.ShapeDtypeStruct((rows, LANES), BF16), jax.ShapeDtypeStruct((8 + 2 * chans, LANES), F32)],
        compiler_params=PARAMS,
        cost_estimate=pl.CostEstimate(flops=400_000, bytes_accessed=400_000, transcendentals=0),
        name="side",
    )(short_taps, query_in, w_out)
    group = [members(devices)]
    message = lax.all_to_all(message, "seq", 0, 0, axis_index_groups=group)
    spectra, heads = pl.pallas_call(
        functools.partial(middle_kernel, devices),
        in_specs=[SMEM] + [VMEM] * 3,
        out_specs=[VMEM] * 2,
        out_shape=[
            jax.ShapeDtypeStruct((devices, 2 * per, LANES), BF16),
            jax.ShapeDtypeStruct((8, LANES), F32),
        ],
        scratch_shapes=[pltpu.VMEM((2, devices, LANES), F32)] * 2 + [pltpu.VMEM((devices, 4 * per, LANES), F32)],
        compiler_params=PARAMS,
        name="middle",
    )(skip_gain, scalars, message.reshape(-1, LANES), basis)
    spectra = lax.all_to_all(spectra, "seq", 0, 0, axis_index_groups=group)
    gating = pl.pallas_call(
        functools.partial(inverse_kernel, devices),
        in_specs=[VMEM] * 7,
        out_specs=VMEM,
        out_shape=jax.ShapeDtypeStruct((rows, LANES), BF16),
        compiler_params=PARAMS,
        name="inverse",
    )(spectra, turn, inverse_second, inverse_first, q_feat, skipped, heads)
    gathered = [gating] + [
        lax.ppermute(gating, "chan", [(c, c // near * near + (c + step) % near) for c in range(chans)])
        for step in range(1, near)
    ]
    own, other = pl.pallas_call(
        mix_kernel,
        in_specs=[VMEM] * (near + 1),
        out_specs=[VMEM] * 2,
        out_shape=[jax.ShapeDtypeStruct((rows, LANES), F32), jax.ShapeDtypeStruct((rows, LANES), BF16)],
        compiler_params=PARAMS,
        name="mix",
    )(scalars, *gathered)
    other = lax.ppermute(other, "chan", [(c, (c + near) % chans) for c in range(chans)])
    return pl.pallas_call(
        add_kernel,
        in_specs=[VMEM] * 2,
        out_specs=VMEM,
        out_shape=jax.ShapeDtypeStruct((1, width), BF16),
        compiler_params=PARAMS,
        name="add",
    )(own, other)


def solution(mesh):
    return jax.shard_map(
        functools.partial(on_device, mesh.shape["seq"], mesh.shape["chan"]),
        mesh=mesh,
        in_specs=(
            P("chan", "seq"),
            P("chan", "seq"),
            P("chan", "seq"),
            P(None, "chan", None),
            P("chan", "seq"),
            P("chan"),
            P(),
        ),
        out_specs=P("chan", "seq"),
        check_vma=False,
    )
```

```python
import functools
import math

import jax
import jax.numpy as jnp
import ml_dtypes
import numpy as np
from jax import lax
from jax.experimental import pallas as pl
from jax.experimental.pallas import tpu as pltpu
from jax.sharding import PartitionSpec as P

LANES = 128
PACK = 2
CHUNKS = 2
F32 = jnp.float32
BF16 = jnp.bfloat16
VMEM_LIMIT = 40 * 1024 * 1024


def tables(rows, devices):
    length = rows * LANES
    per = rows // devices
    k1 = np.arange(rows)
    first = 2.0 * math.pi * np.outer(k1 + 0.25, np.arange(rows)) / rows
    forward_first = np.stack([np.cos(first), -np.sin(first)])
    forward_first = forward_first.reshape(2, devices, per, rows).transpose(1, 0, 2, 3).reshape(2 * rows, rows)
    inverse_first = np.concatenate([np.cos(first), -np.sin(first)]).T / length
    turn = 2.0 * math.pi * np.outer(k1 + 0.25, np.arange(LANES)) / length
    turn = np.stack([np.cos(turn), np.sin(turn)])
    second = 2.0 * math.pi * np.outer(np.arange(LANES), np.arange(LANES)) / LANES
    cos, sin = np.cos(second), np.sin(second)
    forward_second = np.block([[cos, -sin], [sin, cos]])
    inverse_second = np.block([[cos, sin], [-sin, cos]])
    basis = 2.0 * math.pi * (np.arange(per)[:, None] + 0.25 + rows * np.arange(LANES)[None, :]) / length
    basis = np.stack([np.cos(basis), -np.sin(basis)])
    half = lambda values: values.astype(ml_dtypes.bfloat16)
    return (
        half(forward_first),
        turn.astype(np.float32),
        half(forward_second),
        half(inverse_second),
        half(inverse_first),
        basis.astype(np.float32),
    )


def members(devices):
    if devices != 32:
        return list(range(devices))
    return [x * 8 + z * 2 + core for z in (2, 3, 1, 0) for x in (2, 3, 1, 0) for core in (1, 0)]


def dot(left, right):
    return jnp.dot(left, right, preferred_element_type=F32)


def moved_on(values, lane, row):
    turned = pltpu.roll(values, 1, 1)
    carried = jnp.where(row == 0, 0.0, pltpu.roll(turned, 1, 0))
    return jnp.where(lane == 0, carried, turned)


def featurized(signal, taps, stream):
    lane = lax.broadcasted_iota(jnp.int32, signal.shape, 1)
    row = lax.broadcasted_iota(jnp.int32, signal.shape, 0)
    once = moved_on(signal, lane, row)
    twice = moved_on(once, lane, row)
    summed = taps[stream][0] * signal + taps[stream][1] * once + taps[stream][2] * twice
    return summed.astype(BF16)


def at_lanes(values, first):
    return pltpu.roll(values, first, 1) if first else values


def forward_kernel(devices, taps_hbm, k_hbm, v_hbm, q_hbm, filter_hbm, first_hbm, turn_hbm, second_hbm,
                   message_hbm, product_ref,
                   taps_ref, k_ref, v_ref, q_ref, filter_ref, first_ref, turn_ref, second_ref, sems, message_ref, out_sems):
    width = k_hbm.shape[1]
    pairs = (
        (taps_hbm, taps_ref),
        (k_hbm, k_ref),
        (v_hbm, v_ref),
        (filter_hbm, filter_ref),
        (first_hbm, first_ref),
        (q_hbm.at[:, pl.ds(0, LANES)], q_ref.at[0]),
        (q_hbm.at[:, pl.ds(width - LANES, LANES)], q_ref.at[1]),
        (turn_hbm, turn_ref),
        (second_hbm, second_ref),
    )
    copies = [pltpu.make_async_copy(source, target, sems.at[i]) for i, (source, target) in enumerate(pairs)]
    for copy in copies:
        copy.start()
    rows = product_ref.shape[0]
    per = rows // devices
    lane = lax.broadcasted_iota(jnp.int32, (1, LANES), 1)
    copies[0].wait()
    taps = [[taps_ref[stream, :, j : j + 1] for j in range(3)] for stream in range(3)]
    for copy in copies[1:]:
        copy.wait()
    key = k_ref[...].astype(F32).reshape(rows, LANES)
    k_feat = featurized(key, taps, 1)
    value = v_ref[...].astype(F32).reshape(rows, LANES)
    v_feat = featurized(value, taps, 2)
    product = k_feat.astype(F32) * v_feat.astype(F32)
    product_ref[...] = product
    signals = jnp.concatenate([product, filter_ref[...]], axis=1).astype(BF16)
    values = dot(first_ref[...], signals).reshape(devices, 2, per, 2 * LANES)
    edges = jnp.zeros((1, LANES), F32)
    pieces = ((key[:1], key[rows - 1 :]), (value[:1], value[rows - 1 :]), (q_ref[0].astype(F32), q_ref[1].astype(F32)))
    for i, (head, tail) in enumerate(pieces):
        ends = jnp.where(lane < 2, head, jnp.where(lane < LANES - 2, 0.0, tail))
        edges = edges + at_lanes(ends, 4 * i)
    row = lax.broadcasted_iota(jnp.int32, (8, LANES), 0)
    edges = jnp.where(row == 0, jnp.broadcast_to(edges, (8, LANES)), 0.0)[:PACK].astype(BF16)
    packs = 4 * per // PACK
    count = devices // CHUNKS
    for chunk in range(CHUNKS):
        part = slice(chunk * count, (chunk + 1) * count)
        lines = slice(chunk * count * per, (chunk + 1) * count * per)
        real, imag = values[part, 0], values[part, 1]
        turn_real = turn_ref[0, lines].reshape(count, per, LANES)
        turn_imag = turn_ref[1, lines].reshape(count, per, LANES)
        packed = []
        for signal in range(2):
            lanes = slice(signal * LANES, (signal + 1) * LANES)
            a, b = real[:, :, lanes], imag[:, :, lanes]
            packed.append(
                jnp.concatenate([a * turn_real + b * turn_imag, b * turn_real - a * turn_imag], axis=2)
            )
        packed = jnp.concatenate(packed, axis=1).reshape(2 * count * per, 2 * LANES).astype(BF16)
        spectra = dot(packed, second_ref[...]).reshape(count, 2 * per, 2 * LANES)
        spectra = jnp.concatenate(
            [
                spectra[:, :per, :LANES],
                spectra[:, :per, LANES:],
                spectra[:, per:, :LANES],
                spectra[:, per:, LANES:],
            ],
            axis=1,
        ).astype(BF16)
        message_ref[part, :packs] = spectra.reshape(count, packs, PACK, LANES)
        message_ref[part, packs] = jnp.broadcast_to(edges[None], (count, PACK, LANES))
        copies.append(pltpu.make_async_copy(message_ref.at[part], message_hbm.at[part], out_sems.at[chunk]))
        copies[-1].start()
    for copy in copies[9:]:
        copy.wait()


def side_kernel(devices, taps_ref, q_ref, w_ref, q_feat_ref, scalars_ref):
    rows = q_feat_ref.shape[0]
    own_chan = lax.axis_index("chan")
    lane = lax.broadcasted_iota(jnp.int32, (1, LANES), 1)
    taps = [[taps_ref[stream, :, j : j + 1] for j in range(3)] for stream in range(3)]
    for j in range(3):
        scalars_ref[j : j + 1, :] = jnp.where(lane < 4, taps[1][j], jnp.where(lane < 8, taps[2][j], taps[0][j]))
    query = q_ref[...].astype(F32).reshape(rows, LANES)
    q_feat_ref[...] = featurized(query, taps, 0)
    chans = w_ref.shape[0]
    weights = w_ref[...].astype(F32)
    row = lax.broadcasted_iota(jnp.int32, weights.shape, 0)
    for half in range(2):
        chan = (own_chan + half * (chans // 2)) % chans
        picked = jnp.sum(jnp.where(row == chan, weights, 0.0), axis=0, keepdims=True)
        for d in range(chans):
            index = 8 + half * chans + d
            scalars_ref[index : index + 1, :] = jnp.broadcast_to(picked[:, d : d + 1], (1, LANES))


def rounded(values):
    return values.astype(BF16).astype(F32)


def middle_kernel(devices, skip_ref, scalars_ref, message_ref, basis_ref, out_ref, heads_ref, heads_scratch, error_scratch, aligned_ref):
    pitch = message_ref.shape[0] // devices
    per = (pitch - PACK) // 4
    message = message_ref[...].astype(F32)
    own = lax.axis_index("seq")
    order = members(devices)
    own_slice = sum(jnp.where(own == device, i, 0) for i, device in enumerate(order))
    slabs = [order.index(p) * pitch for p in range(devices)]
    edges = jnp.concatenate([message[slab + 4 * per : slab + 4 * per + 1] for slab in slabs], axis=0)
    before = jnp.concatenate([jnp.zeros((1, LANES), F32), edges[:-1]], axis=0)
    lane = lax.broadcasted_iota(jnp.int32, edges.shape, 1)
    taps = [scalars_ref[j : j + 1, :] for j in range(3)]
    once = pltpu.roll(edges, 1, 1)
    alone = taps[0] * edges + taps[1] * jnp.where(lane % 4 == 0, 0.0, once)
    once = jnp.where(lane % 4 == 0, pltpu.roll(before, 1, 1), once)
    heads = rounded(taps[0] * edges + taps[1] * once + taps[2] * pltpu.roll(before, 2, 1))
    alone = rounded(alone)
    product = heads * pltpu.roll(heads, LANES - 4, 1)
    error = product - alone * pltpu.roll(alone, LANES - 4, 1)
    error = jnp.where(lax.broadcasted_iota(jnp.int32, edges.shape, 0) == 0, 0.0, error)
    for i in range(2):
        error_scratch[i] = jnp.broadcast_to(error[:, i : i + 1], edges.shape)
    heads_scratch[0] = pltpu.roll(heads, LANES - 8, 1)
    heads_scratch[1] = product
    for i in range(2):
        heads_ref[i : i + 1, :] = heads_scratch[i, pl.ds(own, 1), :]
    heads_ref[2:3, :] = jnp.full((1, LANES), skip_ref[0], F32)
    angle = jnp.full((per, LANES), own_slice, jnp.int32).astype(F32) * (2.0 * math.pi / (devices * LANES))
    square = angle * angle
    cos = 1.0 - square * (0.5 - square * (1.0 / 24.0))
    sin = angle * (1.0 - square * (1.0 / 6.0 - square * (1.0 / 120.0)))
    basis_real, basis_imag = basis_ref[0], basis_ref[1]
    point_real = basis_real * cos + basis_imag * sin
    point_imag = basis_imag * cos - basis_real * sin
    blocks = []
    for p in range(devices):
        aligned_ref[p] = message[slabs[p] : slabs[p] + 4 * per]
    for p in range(devices):
        block = aligned_ref[p]
        real, imag = block[:per], block[per : 2 * per]
        if p > 0:
            first = error_scratch[1, p : p + 1, :]
            real = real + (error_scratch[0, p : p + 1, :] + first * point_real)
            imag = imag + first * point_imag
        c, d = block[2 * per : 3 * per], block[3 * per : 4 * per]
        blocks.append((real + imag, real, imag, c, d - c, c + d))
    behind_real = jnp.zeros((per, LANES), F32)
    behind_imag = behind_real
    for p in range(devices):
        sums = [None] * 3
        for q in range(p + 1):
            for i in range(3):
                term = blocks[q][i] * blocks[p - q][3 + i]
                sums[i] = term if sums[i] is None else sums[i] + term
        real, imag = sums[0] - sums[2], sums[0] + sums[1]
        out_ref[order.index(p)] = jnp.concatenate([real - behind_imag, imag + behind_real], axis=0).astype(BF16)
        behind_real, behind_imag = real, imag


def inverse_kernel(devices, spectra_ref, turn_ref, second_ref, first_ref, q_feat_ref, skipped_ref, heads_ref, gating_ref):
    rows = q_feat_ref.shape[0]
    per = rows // devices
    packed = jnp.concatenate(
        [spectra_ref[:, :per, :].astype(F32), spectra_ref[:, per:, :].astype(F32)], axis=2
    )
    values = dot(packed.reshape(rows, 2 * LANES).astype(BF16), second_ref[...])
    a, b = values[:, :LANES], values[:, LANES:]
    turn_real, turn_imag = turn_ref[0], turn_ref[1]
    turned = jnp.concatenate([a * turn_real - b * turn_imag, a * turn_imag + b * turn_real], axis=0)
    convolved = dot(first_ref[...], turned.astype(BF16))
    lane = lax.broadcasted_iota(jnp.int32, (rows, LANES), 1)
    row = lax.broadcasted_iota(jnp.int32, (rows, LANES), 0)
    head = (row == 0) & (lane < 2)
    q_feat = jnp.where(head, heads_ref[0:1, :], q_feat_ref[...].astype(F32))
    skipped = heads_ref[2:3, :] * jnp.where(head, heads_ref[1:2, :], skipped_ref[...])
    gating = (q_feat * (convolved + skipped)).astype(BF16)
    gating_ref[...] = gating


def mix_kernel(scalars_ref, own_gating_ref, other_gating_ref, own_ref, *message_refs):
    near = len(message_refs) + 1
    own_chan = lax.axis_index("chan")
    own, other = own_gating_ref[...].astype(F32), other_gating_ref[...].astype(F32)
    for step in range(near):
        to = 8 + own_chan // near * near + (own_chan + step) % near
        total = scalars_ref[pl.ds(to, 1), :] * own + scalars_ref[pl.ds(to + 2 * near, 1), :] * other
        if step == 0:
            own_ref[...] = total
        else:
            message_refs[step - 1][...] = total.astype(BF16)


def add_kernel(own_ref, *refs):
    *message_refs, out_ref = refs
    total = own_ref[...]
    for message_ref in message_refs:
        total = total + message_ref[...].astype(F32)
    out_ref[...] = total.reshape(out_ref.shape).astype(BF16)


SMEM = pl.BlockSpec(memory_space=pltpu.SMEM)
VMEM = pl.BlockSpec(memory_space=pltpu.VMEM)
HBM = pl.BlockSpec(memory_space=pltpu.HBM)
PARAMS = pltpu.CompilerParams(vmem_limit_bytes=VMEM_LIMIT)


def on_device(devices, chans, query_in, key_in, value_in, short_taps, long_filter, skip_gain, w_out):
    width = query_in.shape[1]
    rows = width // LANES
    per = rows // devices
    near = chans // 2
    forward_first, turn, forward_second, inverse_second, inverse_first, basis = tables(rows, devices)
    message_shape = (devices, 4 * per // PACK + 1, PACK, LANES)
    message, skipped = pl.pallas_call(
        functools.partial(forward_kernel, devices),
        in_specs=[HBM] * 8,
        out_specs=[HBM, VMEM],
        out_shape=[jax.ShapeDtypeStruct(message_shape, BF16), jax.ShapeDtypeStruct((rows, LANES), F32)],
        scratch_shapes=[
            pltpu.VMEM(short_taps.shape, F32),
            pltpu.VMEM((1, width), BF16),
            pltpu.VMEM((1, width), BF16),
            pltpu.VMEM((2, 1, LANES), BF16),
            pltpu.VMEM((rows, LANES), F32),
            pltpu.VMEM(forward_first.shape, BF16),
            pltpu.VMEM(turn.shape, F32),
            pltpu.VMEM(forward_second.shape, BF16),
            pltpu.SemaphoreType.DMA((9,)),
            pltpu.VMEM(message_shape, BF16),
            pltpu.SemaphoreType.DMA((CHUNKS,)),
        ],
        compiler_params=PARAMS,
        name="forward",
    )(
        *(
            pltpu.with_memory_space_constraint(jnp.asarray(operand), pltpu.HBM)
            for operand in (
                short_taps, key_in, value_in, query_in, long_filter.reshape(rows, LANES),
                forward_first, turn, forward_second,
            )
        ),
    )
    q_feat, scalars = pl.pallas_call(
        functools.partial(side_kernel, devices),
        in_specs=[VMEM] * 3,
        out_specs=[VMEM] * 2,
        out_shape=[jax.ShapeDtypeStruct((rows, LANES), BF16), jax.ShapeDtypeStruct((8 + 2 * chans, LANES), F32)],
        compiler_params=PARAMS,
        cost_estimate=pl.CostEstimate(flops=400_000, bytes_accessed=400_000, transcendentals=0),
        name="side",
    )(short_taps, query_in, w_out)
    group = [members(devices)]
    message = lax.all_to_all(message, "seq", 0, 0, axis_index_groups=group)
    spectra, heads = pl.pallas_call(
        functools.partial(middle_kernel, devices),
        in_specs=[SMEM] + [VMEM] * 3,
        out_specs=[VMEM] * 2,
        out_shape=[
            jax.ShapeDtypeStruct((devices, 2 * per, LANES), BF16),
            jax.ShapeDtypeStruct((8, LANES), F32),
        ],
        scratch_shapes=[pltpu.VMEM((2, devices, LANES), F32)] * 2 + [pltpu.VMEM((devices, 4 * per, LANES), F32)],
        compiler_params=PARAMS,
        name="middle",
    )(skip_gain, scalars, message.reshape(-1, LANES), basis)
    spectra = lax.all_to_all(spectra, "seq", 0, 0, axis_index_groups=group)
    gating = pl.pallas_call(
        functools.partial(inverse_kernel, devices),
        in_specs=[VMEM] * 7,
        out_specs=VMEM,
        out_shape=jax.ShapeDtypeStruct((rows, LANES), BF16),
        compiler_params=PARAMS,
        name="inverse",
    )(spectra, turn, inverse_second, inverse_first, q_feat, skipped, heads)
    other_gating = lax.ppermute(gating, "chan", [(c, (c + near) % chans) for c in range(chans)])
    own, *messages = pl.pallas_call(
        mix_kernel,
        in_specs=[VMEM] * 3,
        out_specs=[VMEM] * near,
        out_shape=[jax.ShapeDtypeStruct((rows, LANES), BF16 if step else F32) for step in range(near)],
        compiler_params=PARAMS,
        name="mix",
    )(scalars, gating, other_gating)
    messages = [
        lax.ppermute(message, "chan", [(c, c // near * near + (c + step) % near) for c in range(chans)])
        for step, message in enumerate(messages, 1)
    ]
    return pl.pallas_call(
        add_kernel,
        in_specs=[VMEM] * near,
        out_specs=VMEM,
        out_shape=jax.ShapeDtypeStruct((1, width), BF16),
        compiler_params=PARAMS,
        name="add",
    )(own, *messages)


def solution(mesh):
    return jax.shard_map(
        functools.partial(on_device, mesh.shape["seq"], mesh.shape["chan"]),
        mesh=mesh,
        in_specs=(
            P("chan", "seq"),
            P("chan", "seq"),
            P("chan", "seq"),
            P(None, "chan", None),
            P("chan", "seq"),
            P("chan"),
            P(),
        ),
        out_specs=P("chan", "seq"),
        check_vma=False,
    )
```

```python
import functools
import math

import jax
import jax.numpy as jnp
import ml_dtypes
import numpy as np
from jax import lax
from jax.experimental import pallas as pl
from jax.experimental.pallas import tpu as pltpu
from jax.sharding import PartitionSpec as P

LANES = 128
PACK = 2
CHUNKS = 2
F32 = jnp.float32
BF16 = jnp.bfloat16
VMEM_LIMIT = 40 * 1024 * 1024


def tables(rows, devices):
    length = rows * LANES
    per = rows // devices
    k1 = np.arange(rows)
    first = 2.0 * math.pi * np.outer(k1 + 0.25, np.arange(rows)) / rows
    forward_first = np.stack([np.cos(first), -np.sin(first)])
    forward_first = forward_first.reshape(2, devices, per, rows).transpose(1, 0, 2, 3).reshape(2 * rows, rows)
    inverse_first = np.concatenate([np.cos(first), -np.sin(first)]).T / length
    turn = 2.0 * math.pi * np.outer(k1 + 0.25, np.arange(LANES)) / length
    turn = np.stack([np.cos(turn), np.sin(turn)])
    second = 2.0 * math.pi * np.outer(np.arange(LANES), np.arange(LANES)) / LANES
    cos, sin = np.cos(second), np.sin(second)
    forward_second = np.block([[cos, -sin], [sin, cos]])
    inverse_second = np.block([[cos, sin], [-sin, cos]])
    basis = 2.0 * math.pi * (np.arange(per)[:, None] + 0.25 + rows * np.arange(LANES)[None, :]) / length
    basis = np.stack([np.cos(basis), -np.sin(basis)])
    half = lambda values: values.astype(ml_dtypes.bfloat16)
    return (
        half(forward_first),
        turn.astype(np.float32),
        half(forward_second),
        half(inverse_second),
        half(inverse_first),
        basis.astype(np.float32),
    )


def members(devices):
    if devices != 32:
        return list(range(devices))
    return [x * 8 + z * 2 + core for z in (2, 3, 1, 0) for x in (2, 3, 1, 0) for core in (1, 0)]


def dot(left, right):
    return jnp.dot(left, right, preferred_element_type=F32)


def moved_on(values, lane, row):
    turned = pltpu.roll(values, 1, 1)
    carried = jnp.where(row == 0, 0.0, pltpu.roll(turned, 1, 0))
    return jnp.where(lane == 0, carried, turned)


def featurized(signal, taps, stream):
    lane = lax.broadcasted_iota(jnp.int32, signal.shape, 1)
    row = lax.broadcasted_iota(jnp.int32, signal.shape, 0)
    once = moved_on(signal, lane, row)
    twice = moved_on(once, lane, row)
    summed = taps[stream][0] * signal + taps[stream][1] * once + taps[stream][2] * twice
    return summed.astype(BF16)


def at_lanes(values, first):
    return pltpu.roll(values, first, 1) if first else values


def forward_kernel(devices, taps_hbm, k_hbm, v_hbm, q_hbm, filter_hbm, first_hbm, turn_hbm, second_hbm,
                   message_hbm, product_ref,
                   taps_ref, k_ref, v_ref, q_ref, filter_ref, first_ref, turn_ref, second_ref, sems, message_ref, out_sems):
    width = k_hbm.shape[1]
    pairs = (
        (taps_hbm, taps_ref),
        (k_hbm, k_ref),
        (v_hbm, v_ref),
        (filter_hbm, filter_ref),
        (first_hbm, first_ref),
        (q_hbm.at[:, pl.ds(0, LANES)], q_ref.at[0]),
        (q_hbm.at[:, pl.ds(width - LANES, LANES)], q_ref.at[1]),
        (turn_hbm, turn_ref),
        (second_hbm, second_ref),
    )
    copies = [pltpu.make_async_copy(source, target, sems.at[i]) for i, (source, target) in enumerate(pairs)]
    for copy in copies:
        copy.start()
    rows = product_ref.shape[0]
    per = rows // devices
    lane = lax.broadcasted_iota(jnp.int32, (1, LANES), 1)
    copies[0].wait()
    taps = [[taps_ref[stream, :, j : j + 1] for j in range(3)] for stream in range(3)]
    for copy in copies[1:3]:
        copy.wait()
    key = k_ref[...].astype(F32).reshape(rows, LANES)
    k_feat = featurized(key, taps, 1)
    value = v_ref[...].astype(F32).reshape(rows, LANES)
    v_feat = featurized(value, taps, 2)
    product = k_feat.astype(F32) * v_feat.astype(F32)
    product_ref[...] = product
    for copy in copies[3:]:
        copy.wait()
    signals = jnp.concatenate([product, filter_ref[...]], axis=1).astype(BF16)
    values = dot(first_ref[...], signals).reshape(devices, 2, per, 2 * LANES)
    edges = jnp.zeros((1, LANES), F32)
    pieces = ((key[:1], key[rows - 1 :]), (value[:1], value[rows - 1 :]), (q_ref[0].astype(F32), q_ref[1].astype(F32)))
    for i, (head, tail) in enumerate(pieces):
        ends = jnp.where(lane < 2, head, jnp.where(lane < LANES - 2, 0.0, tail))
        edges = edges + at_lanes(ends, 4 * i)
    row = lax.broadcasted_iota(jnp.int32, (8, LANES), 0)
    edges = jnp.where(row == 0, jnp.broadcast_to(edges, (8, LANES)), 0.0)[:PACK].astype(BF16)
    packs = 4 * per // PACK
    count = devices // CHUNKS
    for chunk in range(CHUNKS):
        part = slice(chunk * count, (chunk + 1) * count)
        lines = slice(chunk * count * per, (chunk + 1) * count * per)
        real, imag = values[part, 0], values[part, 1]
        turn_real = turn_ref[0, lines].reshape(count, per, LANES)
        turn_imag = turn_ref[1, lines].reshape(count, per, LANES)
        packed = []
        for signal in range(2):
            lanes = slice(signal * LANES, (signal + 1) * LANES)
            a, b = real[:, :, lanes], imag[:, :, lanes]
            packed.append(
                jnp.concatenate([a * turn_real + b * turn_imag, b * turn_real - a * turn_imag], axis=2)
            )
        packed = jnp.concatenate(packed, axis=1).reshape(2 * count * per, 2 * LANES).astype(BF16)
        spectra = dot(packed, second_ref[...]).reshape(count, 2 * per, 2 * LANES)
        spectra = jnp.concatenate(
            [
                spectra[:, :per, :LANES],
                spectra[:, :per, LANES:],
                spectra[:, per:, :LANES],
                spectra[:, per:, LANES:],
            ],
            axis=1,
        ).astype(BF16)
        message_ref[part, :packs] = spectra.reshape(count, packs, PACK, LANES)
        message_ref[part, packs] = jnp.broadcast_to(edges[None], (count, PACK, LANES))
        copies.append(pltpu.make_async_copy(message_ref.at[part], message_hbm.at[part], out_sems.at[chunk]))
        copies[-1].start()
    for copy in copies[9:]:
        copy.wait()


def side_kernel(devices, taps_ref, q_ref, w_ref, q_feat_ref, scalars_ref):
    rows = q_feat_ref.shape[0]
    own_chan = lax.axis_index("chan")
    lane = lax.broadcasted_iota(jnp.int32, (1, LANES), 1)
    taps = [[taps_ref[stream, :, j : j + 1] for j in range(3)] for stream in range(3)]
    for j in range(3):
        scalars_ref[j : j + 1, :] = jnp.where(lane < 4, taps[1][j], jnp.where(lane < 8, taps[2][j], taps[0][j]))
    query = q_ref[...].astype(F32).reshape(rows, LANES)
    q_feat_ref[...] = featurized(query, taps, 0)
    chans = w_ref.shape[0]
    weights = w_ref[...].astype(F32)
    row = lax.broadcasted_iota(jnp.int32, weights.shape, 0)
    for half in range(2):
        chan = (own_chan + half * (chans // 2)) % chans
        picked = jnp.sum(jnp.where(row == chan, weights, 0.0), axis=0, keepdims=True)
        for d in range(chans):
            index = 8 + half * chans + d
            scalars_ref[index : index + 1, :] = jnp.broadcast_to(picked[:, d : d + 1], (1, LANES))


def rounded(values):
    return values.astype(BF16).astype(F32)


def middle_kernel(devices, skip_ref, scalars_ref, message_ref, basis_ref, out_ref, heads_ref, heads_scratch, error_scratch, aligned_ref):
    pitch = message_ref.shape[0] // devices
    per = (pitch - PACK) // 4
    message = message_ref[...].astype(F32)
    own = lax.axis_index("seq")
    order = members(devices)
    own_slice = sum(jnp.where(own == device, i, 0) for i, device in enumerate(order))
    slabs = [order.index(p) * pitch for p in range(devices)]
    edges = jnp.concatenate([message[slab + 4 * per : slab + 4 * per + 1] for slab in slabs], axis=0)
    before = jnp.concatenate([jnp.zeros((1, LANES), F32), edges[:-1]], axis=0)
    lane = lax.broadcasted_iota(jnp.int32, edges.shape, 1)
    taps = [scalars_ref[j : j + 1, :] for j in range(3)]
    once = pltpu.roll(edges, 1, 1)
    alone = taps[0] * edges + taps[1] * jnp.where(lane % 4 == 0, 0.0, once)
    once = jnp.where(lane % 4 == 0, pltpu.roll(before, 1, 1), once)
    heads = rounded(taps[0] * edges + taps[1] * once + taps[2] * pltpu.roll(before, 2, 1))
    alone = rounded(alone)
    product = heads * pltpu.roll(heads, LANES - 4, 1)
    error = product - alone * pltpu.roll(alone, LANES - 4, 1)
    error = jnp.where(lax.broadcasted_iota(jnp.int32, edges.shape, 0) == 0, 0.0, error)
    for i in range(2):
        error_scratch[i] = jnp.broadcast_to(error[:, i : i + 1], edges.shape)
    heads_scratch[0] = pltpu.roll(heads, LANES - 8, 1)
    heads_scratch[1] = product
    for i in range(2):
        heads_ref[i : i + 1, :] = heads_scratch[i, pl.ds(own, 1), :]
    heads_ref[2:3, :] = jnp.full((1, LANES), skip_ref[0], F32)
    angle = jnp.full((per, LANES), own_slice, jnp.int32).astype(F32) * (2.0 * math.pi / (devices * LANES))
    square = angle * angle
    cos = 1.0 - square * (0.5 - square * (1.0 / 24.0))
    sin = angle * (1.0 - square * (1.0 / 6.0 - square * (1.0 / 120.0)))
    basis_real, basis_imag = basis_ref[0], basis_ref[1]
    point_real = basis_real * cos + basis_imag * sin
    point_imag = basis_imag * cos - basis_real * sin
    blocks = []
    for p in range(devices):
        aligned_ref[p] = message[slabs[p] : slabs[p] + 4 * per]
    for p in range(devices):
        block = aligned_ref[p]
        real, imag = block[:per], block[per : 2 * per]
        if p > 0:
            first = error_scratch[1, p : p + 1, :]
            real = real + (error_scratch[0, p : p + 1, :] + first * point_real)
            imag = imag + first * point_imag
        c, d = block[2 * per : 3 * per], block[3 * per : 4 * per]
        blocks.append((real + imag, real, imag, c, d - c, c + d))
    behind_real = jnp.zeros((per, LANES), F32)
    behind_imag = behind_real
    for p in range(devices):
        sums = [None] * 3
        for q in range(p + 1):
            for i in range(3):
                term = blocks[q][i] * blocks[p - q][3 + i]
                sums[i] = term if sums[i] is None else sums[i] + term
        real, imag = sums[0] - sums[2], sums[0] + sums[1]
        out_ref[order.index(p)] = jnp.concatenate([real - behind_imag, imag + behind_real], axis=0).astype(BF16)
        behind_real, behind_imag = real, imag


def inverse_kernel(devices, spectra_ref, turn_ref, second_ref, first_ref, q_feat_ref, skipped_ref, heads_ref, gating_ref):
    rows = q_feat_ref.shape[0]
    per = rows // devices
    packed = jnp.concatenate(
        [spectra_ref[:, :per, :].astype(F32), spectra_ref[:, per:, :].astype(F32)], axis=2
    )
    values = dot(packed.reshape(rows, 2 * LANES).astype(BF16), second_ref[...])
    a, b = values[:, :LANES], values[:, LANES:]
    turn_real, turn_imag = turn_ref[0], turn_ref[1]
    turned = jnp.concatenate([a * turn_real - b * turn_imag, a * turn_imag + b * turn_real], axis=0)
    convolved = dot(first_ref[...], turned.astype(BF16))
    lane = lax.broadcasted_iota(jnp.int32, (rows, LANES), 1)
    row = lax.broadcasted_iota(jnp.int32, (rows, LANES), 0)
    head = (row == 0) & (lane < 2)
    q_feat = jnp.where(head, heads_ref[0:1, :], q_feat_ref[...].astype(F32))
    skipped = heads_ref[2:3, :] * jnp.where(head, heads_ref[1:2, :], skipped_ref[...])
    gating = (q_feat * (convolved + skipped)).astype(BF16)
    gating_ref[...] = gating


def mix_kernel(scalars_ref, own_gating_ref, other_gating_ref, own_ref, *message_refs):
    near = len(message_refs) + 1
    own_chan = lax.axis_index("chan")
    own, other = own_gating_ref[...].astype(F32), other_gating_ref[...].astype(F32)
    for step in range(near):
        to = 8 + own_chan // near * near + (own_chan + step) % near
        total = scalars_ref[pl.ds(to, 1), :] * own + scalars_ref[pl.ds(to + 2 * near, 1), :] * other
        if step == 0:
            own_ref[...] = total
        else:
            message_refs[step - 1][...] = total.astype(BF16)


def add_kernel(own_ref, *refs):
    *message_refs, out_ref = refs
    total = own_ref[...]
    for message_ref in message_refs:
        total = total + message_ref[...].astype(F32)
    out_ref[...] = total.reshape(out_ref.shape).astype(BF16)


SMEM = pl.BlockSpec(memory_space=pltpu.SMEM)
VMEM = pl.BlockSpec(memory_space=pltpu.VMEM)
HBM = pl.BlockSpec(memory_space=pltpu.HBM)
PARAMS = pltpu.CompilerParams(vmem_limit_bytes=VMEM_LIMIT)


def on_device(devices, chans, query_in, key_in, value_in, short_taps, long_filter, skip_gain, w_out):
    width = query_in.shape[1]
    rows = width // LANES
    per = rows // devices
    near = chans // 2
    forward_first, turn, forward_second, inverse_second, inverse_first, basis = tables(rows, devices)
    message_shape = (devices, 4 * per // PACK + 1, PACK, LANES)
    message, skipped = pl.pallas_call(
        functools.partial(forward_kernel, devices),
        in_specs=[HBM] * 8,
        out_specs=[HBM, VMEM],
        out_shape=[jax.ShapeDtypeStruct(message_shape, BF16), jax.ShapeDtypeStruct((rows, LANES), F32)],
        scratch_shapes=[
            pltpu.VMEM(short_taps.shape, F32),
            pltpu.VMEM((1, width), BF16),
            pltpu.VMEM((1, width), BF16),
            pltpu.VMEM((2, 1, LANES), BF16),
            pltpu.VMEM((rows, LANES), F32),
            pltpu.VMEM(forward_first.shape, BF16),
            pltpu.VMEM(turn.shape, F32),
            pltpu.VMEM(forward_second.shape, BF16),
            pltpu.SemaphoreType.DMA((9,)),
            pltpu.VMEM(message_shape, BF16),
            pltpu.SemaphoreType.DMA((CHUNKS,)),
        ],
        compiler_params=PARAMS,
        name="forward",
    )(
        *(
            pltpu.with_memory_space_constraint(jnp.asarray(operand), pltpu.HBM)
            for operand in (
                short_taps, key_in, value_in, query_in, long_filter.reshape(rows, LANES),
                forward_first, turn, forward_second,
            )
        ),
    )
    q_feat, scalars = pl.pallas_call(
        functools.partial(side_kernel, devices),
        in_specs=[VMEM] * 3,
        out_specs=[VMEM] * 2,
        out_shape=[jax.ShapeDtypeStruct((rows, LANES), BF16), jax.ShapeDtypeStruct((8 + 2 * chans, LANES), F32)],
        compiler_params=PARAMS,
        cost_estimate=pl.CostEstimate(flops=400_000, bytes_accessed=400_000, transcendentals=0),
        name="side",
    )(short_taps, query_in, w_out)
    group = [members(devices)]
    message = lax.all_to_all(message, "seq", 0, 0, axis_index_groups=group)
    spectra, heads = pl.pallas_call(
        functools.partial(middle_kernel, devices),
        in_specs=[SMEM] + [VMEM] * 3,
        out_specs=[VMEM] * 2,
        out_shape=[
            jax.ShapeDtypeStruct((devices, 2 * per, LANES), BF16),
            jax.ShapeDtypeStruct((8, LANES), F32),
        ],
        scratch_shapes=[pltpu.VMEM((2, devices, LANES), F32)] * 2 + [pltpu.VMEM((devices, 4 * per, LANES), F32)],
        compiler_params=PARAMS,
        name="middle",
    )(skip_gain, scalars, message.reshape(-1, LANES), basis)
    spectra = lax.all_to_all(spectra, "seq", 0, 0, axis_index_groups=group)
    gating = pl.pallas_call(
        functools.partial(inverse_kernel, devices),
        in_specs=[VMEM] * 7,
        out_specs=VMEM,
        out_shape=jax.ShapeDtypeStruct((rows, LANES), BF16),
        compiler_params=PARAMS,
        name="inverse",
    )(spectra, turn, inverse_second, inverse_first, q_feat, skipped, heads)
    other_gating = lax.ppermute(gating, "chan", [(c, (c + near) % chans) for c in range(chans)])
    own, *messages = pl.pallas_call(
        mix_kernel,
        in_specs=[VMEM] * 3,
        out_specs=[VMEM] * near,
        out_shape=[jax.ShapeDtypeStruct((rows, LANES), BF16 if step else F32) for step in range(near)],
        compiler_params=PARAMS,
        name="mix",
    )(scalars, gating, other_gating)
    messages = [
        lax.ppermute(message, "chan", [(c, c // near * near + (c + step) % near) for c in range(chans)])
        for step, message in enumerate(messages, 1)
    ]
    return pl.pallas_call(
        add_kernel,
        in_specs=[VMEM] * near,
        out_specs=VMEM,
        out_shape=jax.ShapeDtypeStruct((1, width), BF16),
        compiler_params=PARAMS,
        name="add",
    )(own, *messages)


def solution(mesh):
    return jax.shard_map(
        functools.partial(on_device, mesh.shape["seq"], mesh.shape["chan"]),
        mesh=mesh,
        in_specs=(
            P("chan", "seq"),
            P("chan", "seq"),
            P("chan", "seq"),
            P(None, "chan", None),
            P("chan", "seq"),
            P("chan"),
            P(),
        ),
        out_specs=P("chan", "seq"),
        check_vma=False,
    )
```
